32 devices in a mesh: seq: 8 (over z, x), chan: 4 (over y, core).
Axes of the slice: x: 2, y: 2, z: 4, core: 2. Of those that a mesh axis runs over, the one named last changes fastest.
Arguments:
- tokens: bfloat16 [1024, 4096], P('seq'), may hold values from -6 to 6
- w_inner: bfloat16 [4096, 4096], P('seq', 'chan'), may hold values from -0.09375 to 0.09375
- w_keyquery: bfloat16 [4096, 4, 32], P('seq', 'chan'), may hold values from -0.09375 to 0.09375
- rate: float32 [4096], P('chan'), may hold values from 0.00048828125 to 0.05
- grad_out: bfloat16 [1024, 4096], P('seq', 'chan'), may hold values from -6 to 6
Outputs:
- mixed: bfloat16 [1024, 4096], P('seq', 'chan')
- grad_tokens: bfloat16 [1024, 4096], P('seq', 'chan')
- grad_keyquery: float32 [4096, 4, 32], P('seq', 'chan')
The draws below stay inside these ranges and needn't reach their ends.
All inputs are finite; a program needn't handle non-finite values.
Results may differ from the reference program's by a relative error of at most 0.0049.
Values may be sent and summed in bfloat16 or wider, within the bound.
No kernel may reach another device: no remote copies, remote signals or barrier semaphores. Data moves between devices by JAX's collectives and lax.ppermute only.
A program may use at most 128 MiB of HBM per device.

```python
import math
import jax
import jax.numpy as jnp
from jax import lax

D = 4096
DI = 4096
NS = 16
TOK_DEV = 128
TOKENS = 1024
GROUPS = 4


def steps_of(key, extent, shards, least, top_value):
    factor_of = 1.0
    for axis_at, shards_of in shards:
        steps = jax.random.uniform(jax.random.fold_in(jax.random.fold_in(key, 6), axis_at), (shards_of,), jnp.float32, least / len(shards), top_value / len(shards))
        factor_of = factor_of * jnp.repeat(jnp.exp(steps), extent[axis_at] // shards_of).reshape((-1,) + (1,) * (len(extent) - 1 - axis_at))
    return factor_of


def scatter_about(stream_key, shape, scale, bound, split=(), dtype=jnp.bfloat16):
    result = scale * jax.random.normal(stream_key, shape, jnp.float32)
    if split:
        result = result * steps_of(stream_key, shape, split, -0.22, 0.18)
    return jnp.clip(result, -bound, bound).astype(dtype)


def setup_inputs(seed: int = 0) -> dict:
    key_of = jax.random.split(jax.random.key(seed), 6)
    return {
        "tokens": scatter_about(key_of[0], (TOKENS, D), 1.0, 6.0, ((0, 8),)),
        "w_inner": scatter_about(key_of[1], (D, DI), D ** -0.5, 0.09375, ((0, 8), (1, 4))),
        "w_keyquery": scatter_about(key_of[2], (D, GROUPS, 2 * NS), D ** -0.5, 0.09375, ((0, 8), (1, 4))),
        "rate": jnp.clip(jnp.exp(math.log(0.05) - 4.6288867 * jax.random.uniform(key_of[3], (DI,), jnp.float32) ** steps_of(key_of[3], (DI,), ((0, 4),), -0.2, 0.2)), 0.00048828125, 0.05),
        "grad_out": scatter_about(key_of[4], (TOKENS, DI), 1.0, 6.0, ((0, 8), (1, 4))),
    }


def reference(tokens, w_inner, w_keyquery, rate, grad_out):
    inner = jnp.dot(tokens, w_inner, preferred_element_type=jnp.float32)
    kq_flat = w_keyquery.reshape(D, GROUPS * 2 * NS)
    keyquery = jnp.dot(tokens, kq_flat, preferred_element_type=jnp.float32).reshape(TOKENS, GROUPS, 2 * NS)
    width = DI // GROUPS
    beta = rate.reshape(GROUPS, width, 1)

    def mixer(inner_in, kq_in):
        blocks_x = inner_in.reshape(TOKENS // TOK_DEV, TOK_DEV, GROUPS, width)
        blocks_k = kq_in.reshape(TOKENS // TOK_DEV, TOK_DEV, GROUPS, 2 * NS)

        def step(state, row):
            xrow, krow = row
            keys = krow[:, None, :NS]
            queries = krow[:, None, NS:]
            eps = beta / (1.0 + beta * lax.optimization_barrier(jnp.sum(keys * keys, axis=2, keepdims=True)))
            decay = 1.0 - eps * keys * keys
            state = decay * state + eps * xrow[:, :, None] * keys
            return (state, lax.optimization_barrier(jnp.sum(state * queries, axis=2)))

        @jax.checkpoint
        def block(state, blk):
            return lax.scan(step, state, blk)
        start = jnp.zeros((GROUPS, width, NS), jnp.float32)
        final, outputs = lax.scan(block, start, (blocks_x, blocks_k))
        return outputs.reshape(TOKENS, DI)
    mixed_f, backward = jax.vjp(mixer, inner, keyquery)
    grad_inner, grad_kq = backward(grad_out.astype(jnp.float32))
    inner_b = grad_inner.astype(jnp.bfloat16)
    kq_b = grad_kq.reshape(TOKENS, GROUPS * 2 * NS).astype(jnp.bfloat16)
    grad_tokens = jnp.dot(inner_b, w_inner.T, preferred_element_type=jnp.float32)
    grad_tokens = grad_tokens + jnp.dot(kq_b, kq_flat.T, preferred_element_type=jnp.float32)
    grad_keyquery = jnp.dot(tokens.T, kq_b, preferred_element_type=jnp.float32).reshape(D, GROUPS, 2 * NS)
    return (mixed_f.astype(jnp.bfloat16), grad_tokens.astype(jnp.bfloat16), grad_keyquery)
```

```python
import functools

import jax
import jax.numpy as jnp
from jax import lax
from jax.experimental import pallas as pl
from jax.experimental.pallas import tpu as pltpu
from jax.sharding import PartitionSpec as P

NS = 16
LANES = 128
UNROLL = 8
F32 = jnp.float32
BF16 = jnp.bfloat16


def lane_groups(width):
    return [slice(j * LANES, (j + 1) * LANES) for j in range(width // LANES)]


def tile(ref, first, cols):
    return ref[pl.ds(first, UNROLL), cols]


def place(rows, at, value):
    here = lax.broadcasted_iota(jnp.int32, rows.shape, 0) == at
    return jnp.where(here, jnp.broadcast_to(value, rows.shape), rows)


def to_float(src, dst):
    dst[...] = src[...].astype(F32)


def adjoint_totals_kernel(kq, eps, cot, lam_out, decay_out, cot_f):
    tokens, width = eps.shape
    groups = lane_groups(width)
    to_float(cot, cot_f)

    def block(i, carry):
        lams, decays = carry
        first = pl.multiple_of(tokens - (i + 1) * UNROLL, UNROLL)
        steps = [tile(eps, first, cols) for cols in groups]
        cots = [tile(cot_f, first, cols) for cols in groups]
        for j in reversed(range(UNROLL)):
            t = first + j
            keys = kq[t, :NS, :]
            queries = kq[t, NS:, :]
            square = keys * keys
            new_lams, new_decays = [], []
            for lam, total, step, cot_row in zip(lams, decays, steps, cots):
                decay = 1.0 - step[j : j + 1] * square
                new_lams.append(decay * (queries * cot_row[j : j + 1] + lam))
                new_decays.append(total * decay)
            lams, decays = new_lams, new_decays
        return (tuple(lams), tuple(decays))

    zeros = tuple(jnp.zeros((NS, LANES), F32) for _ in groups)
    ones = tuple(jnp.ones((NS, LANES), F32) for _ in groups)
    lams, decays = lax.fori_loop(0, tokens // UNROLL, block, (zeros, ones))
    for lam, total, cols in zip(lams, decays, groups):
        lam_out[:, cols] = lam
        decay_out[:, cols] = total


def adjoint_kernel(kq, eps, cot, start, adj_out, grad_out, cot_f, grad_f):
    tokens, width = eps.shape
    groups = lane_groups(width)
    to_float(cot, cot_f)

    def block(i, lams):
        first = pl.multiple_of(tokens - (i + 1) * UNROLL, UNROLL)
        steps = [tile(eps, first, cols) for cols in groups]
        cots = [tile(cot_f, first, cols) for cols in groups]
        grads = [jnp.zeros((UNROLL, LANES), F32) for _ in groups]
        for j in reversed(range(UNROLL)):
            t = first + j
            keys = kq[t, :NS, :]
            queries = kq[t, NS:, :]
            square = keys * keys
            new_lams = []
            for n, cols in enumerate(groups):
                adj = queries * cots[n][j : j + 1] + lams[n]
                adj_out[t, :, cols] = adj
                grads[n] = place(grads[n], j, jnp.sum(adj * keys, axis=0, keepdims=True))
                new_lams.append((1.0 - steps[n][j : j + 1] * square) * adj)
            lams = new_lams
        for n, cols in enumerate(groups):
            grad_f[pl.ds(first, UNROLL), cols] = steps[n] * grads[n]
        return tuple(lams)

    lax.fori_loop(0, tokens // UNROLL, block, tuple(start[:, cols] for cols in groups))
    grad_out[...] = grad_f[...].astype(BF16)


def state_total_kernel(kq, eps, inner, state_out):
    tokens, width = eps.shape
    groups = lane_groups(width)

    def block(i, states):
        first = pl.multiple_of(i * UNROLL, UNROLL)
        steps = [tile(eps, first, cols) for cols in groups]
        pushes = [tile(inner, first, cols) * step for cols, step in zip(groups, steps)]
        for j in range(UNROLL):
            t = first + j
            keys = kq[t, :NS, :]
            square = keys * keys
            states = [
                (1.0 - step[j : j + 1] * square) * state + push[j : j + 1] * keys
                for state, step, push in zip(states, steps, pushes)
            ]
        return tuple(states)

    zeros = tuple(jnp.zeros((NS, LANES), F32) for _ in groups)
    states = lax.fori_loop(0, tokens // UNROLL, block, zeros)
    for state, cols in zip(states, groups):
        state_out[:, cols] = state


def mixer_kernel(kq, eps, inner, cot, adj_in, start, mixed_out, gkq_out, cot_f, mixed_f, key_acc, query_acc):
    tokens, width = eps.shape
    groups = lane_groups(width)
    to_float(cot, cot_f)

    @pl.when(pl.program_id(0) == 0)
    def _():
        key_acc[...] = jnp.zeros_like(key_acc)
        query_acc[...] = jnp.zeros_like(query_acc)

    def block(i, states):
        first = pl.multiple_of(i * UNROLL, UNROLL)
        steps = [tile(eps, first, cols) for cols in groups]
        inners = [tile(inner, first, cols) for cols in groups]
        pushes = [step * x for step, x in zip(steps, inners)]
        squares = [step * step for step in steps]
        cots = [tile(cot_f, first, cols) for cols in groups]
        outs = [jnp.zeros((UNROLL, LANES), F32) for _ in groups]
        for j in range(UNROLL):
            t = first + j
            keys = kq[t, :NS, :]
            queries = kq[t, NS:, :]
            square = keys * keys
            new_states = []
            key_sum = jnp.zeros((NS, LANES), F32)
            step_sum = jnp.zeros((NS, LANES), F32)
            query_sum = jnp.zeros((NS, LANES), F32)
            for n, cols in enumerate(groups):
                step = steps[n][j : j + 1]
                adj = adj_in[t, :, cols]
                through_decay = keys * (adj * states[n])
                through_both = inners[n][j : j + 1] * adj - through_decay
                key_sum = key_sum + step * (through_both - through_decay)
                step_sum = step_sum + squares[n][j : j + 1] * through_both
                state = (1.0 - step * square) * states[n] + pushes[n][j : j + 1] * keys
                query_sum = query_sum + state * cots[n][j : j + 1]
                outs[n] = place(outs[n], j, jnp.sum(state * queries, axis=0, keepdims=True))
                new_states.append(state)
            states = new_states
            through_step = jnp.sum(keys * step_sum, axis=0, keepdims=True)
            key_acc[t] += key_sum - 2.0 * keys * through_step
            query_acc[t] += query_sum
        for n, cols in enumerate(groups):
            mixed_f[pl.ds(first, UNROLL), cols] = outs[n]
        return tuple(states)

    lax.fori_loop(0, tokens // UNROLL, block, tuple(start[:, cols] for cols in groups))
    mixed_out[...] = mixed_f[...].astype(BF16)

    @pl.when(pl.program_id(0) == pl.num_programs(0) - 1)
    def _():
        ones = jnp.ones((LANES, LANES), F32)
        lane = lax.broadcasted_iota(jnp.int32, (NS, LANES), 1)
        state = lax.broadcasted_iota(jnp.int32, (NS, LANES), 0)

        def spread(acc, first):
            total = jnp.dot(
                acc[...].reshape(tokens * NS, LANES),
                ones,
                preferred_element_type=F32,
                precision=lax.Precision.HIGHEST,
            )
            placed = jnp.where(
                (lane == state + first)[None], total.reshape(tokens, NS, LANES), 0.0
            )
            return jnp.sum(placed, axis=1)

        gkq_out[...] = spread(key_acc, 0) + spread(query_acc, NS)


def call(kernel, tokens, width, block, ins, outs, scratch, args, flops):
    def spec(kind):
        return {
            "kq": pl.BlockSpec((tokens, 2 * NS, LANES), lambda c: (0, 0, 0)),
            "rows": pl.BlockSpec((tokens, block), lambda c: (0, c)),
            "rows16": pl.BlockSpec((tokens, block), lambda c: (0, c)),
            "state": pl.BlockSpec((NS, block), lambda c: (0, c)),
            "states": pl.BlockSpec((tokens, NS, block), lambda c: (0, 0, c)),
            "gkq": pl.BlockSpec((tokens, LANES), lambda c: (0, 0)),
        }[kind]

    def shape(kind):
        return {
            "rows": jax.ShapeDtypeStruct((tokens, width), F32),
            "rows16": jax.ShapeDtypeStruct((tokens, width), BF16),
            "state": jax.ShapeDtypeStruct((NS, width), F32),
            "states": jax.ShapeDtypeStruct((tokens, NS, width), F32),
            "gkq": jax.ShapeDtypeStruct((tokens, LANES), F32),
        }[kind]

    return pl.pallas_call(
        kernel,
        grid=(width // block,),
        in_specs=[spec(kind) for kind in ins],
        out_specs=[spec(kind) for kind in outs],
        out_shape=[shape(kind) for kind in outs],
        scratch_shapes=scratch,
        compiler_params=pltpu.CompilerParams(vmem_limit_bytes=48 * 2**20),
        cost_estimate=pl.CostEstimate(
            flops=flops * tokens * NS * width,
            bytes_accessed=4 * tokens * width * (1 + NS * ("states" in ins + outs)),
            transcendentals=0,
        ),
    )(*args)


def shifted(value, axis, by):
    peers = lax.axis_size(axis)
    pairs = [(i, i + by) for i in range(peers) if 0 <= i + by < peers]
    return lax.ppermute(value, axis, pairs)


def carried(decay, total, sign):
    count = lax.axis_size("seq")
    window, radix = 1, 4
    inc_decay, inc_total = decay, total
    exc_decay, exc_total = None, None
    while window < count:
        last = window * radix >= count
        for j in range(1, radix):
            if window * j >= count:
                break
            far_total = shifted(inc_total, "seq", sign * window * j)
            far_decay = shifted(inc_decay, "seq", sign * window * j)
            if exc_total is None:
                exc_total, exc_decay = far_total, far_decay
            else:
                exc_total = exc_total + exc_decay * far_total
                exc_decay = exc_decay * far_decay
        if not last:
            inc_total = total + decay * exc_total
            inc_decay = decay * exc_decay
        window *= radix
    return exc_total


def gather_columns(value, axis):
    count = lax.axis_size(axis)
    parts = lax.all_to_all(
        jnp.broadcast_to(value[None], (count,) + value.shape), axis, 0, 0, tiled=True
    )
    return jnp.moveaxis(parts, 0, 1).reshape(value.shape[0], count * value.shape[1])


def scatter_sum_columns(value):
    count = lax.axis_size("chan")
    index = lax.axis_index("chan")
    if count & (count - 1):
        return lax.psum_scatter(value, "chan", scatter_dimension=1, tiled=True)
    blocks = jnp.moveaxis(value.reshape(value.shape[0], count, -1), 1, 0)
    offset = 1
    while offset < count:
        pairs = blocks.reshape((-1, 2) + blocks.shape[1:])
        bit = (index // offset) % 2
        mine = lax.dynamic_index_in_dim(pairs, bit, 1, keepdims=False)
        other = lax.dynamic_index_in_dim(pairs, 1 - bit, 1, keepdims=False)
        wire = other if offset == 1 else other.astype(BF16)
        swap = [(i, i ^ offset) for i in range(count)]
        blocks = mine + lax.ppermute(wire, "chan", swap).astype(F32)
        offset *= 2
    return blocks[0]


def per_device(tokens, w_inner, w_keyquery, rate, grad_out):
    count = tokens.shape[0]
    width = w_inner.shape[1]
    kq_cols = w_keyquery.shape[1] * w_keyquery.shape[2]
    seqs, chans = lax.axis_size("seq"), lax.axis_size("chan")
    block = min(width, 512)
    full_inner = lax.all_gather(w_inner, "seq", axis=0, tiled=True)
    full_kq = gather_columns(w_keyquery.reshape(-1, kq_cols).T, "seq")
    keyquery = lax.dot_general(
        tokens, full_kq, (((1,), (1,)), ((), ())), preferred_element_type=F32
    )
    keys = keyquery[:, :NS]
    sumsq = jnp.sum(keys * keys, axis=1)
    eps = rate[None, :] / (1.0 + rate[None, :] * sumsq[:, None])
    spread = jnp.broadcast_to(keyquery[:, :, None], (count, 2 * NS, LANES))
    rows_f = pltpu.VMEM((count, block), F32)
    run = functools.partial(call, tokens=count, width=width, block=block)

    lam, decay = run(
        adjoint_totals_kernel,
        ins=["kq", "rows", "rows16"], outs=["state", "state"], scratch=[rows_f],
        args=(spread, eps, grad_out), flops=8,
    )
    end_adjoint = carried(decay, lam, -1)
    adjoints, inner_grad = run(
        adjoint_kernel,
        ins=["kq", "rows", "rows16", "state"], outs=["states", "rows16"], scratch=[rows_f, rows_f],
        args=(spread, eps, grad_out, end_adjoint), flops=8,
    )
    inner = jnp.dot(tokens, full_inner, preferred_element_type=F32)
    partial_sum = lax.dot_general(
        inner_grad, full_inner, (((1,), (1,)), ((), ())), preferred_element_type=F32
    )
    tokens_sum = scatter_sum_columns(partial_sum)
    (alone_end,) = run(
        state_total_kernel,
        ins=["kq", "rows", "rows"], outs=["state"], scratch=[],
        args=(spread, eps, inner), flops=6,
    )
    start_state = carried(decay, alone_end, 1)
    acc = pltpu.VMEM((count, NS, LANES), F32)
    mixed, kq_grad = run(
        mixer_kernel,
        ins=["kq", "rows", "rows", "rows16", "states", "state"], outs=["rows16", "gkq"],
        scratch=[rows_f, rows_f, acc, acc],
        args=(spread, eps, inner, grad_out, adjoints, start_state), flops=20,
    )
    kq_grad = kq_grad[:, :kq_cols].astype(BF16)

    kq_rows = lax.all_to_all(
        jnp.moveaxis(full_kq.reshape(kq_cols, chans, -1), 1, 0), "chan", 0, 0, tiled=True
    )
    kq_rows = kq_rows.reshape(chans * kq_cols, -1)
    all_kq = gather_columns(kq_grad, "chan")
    grad_tokens = (
        tokens_sum + jnp.dot(all_kq, kq_rows, preferred_element_type=F32)
    ).astype(BF16)

    grad_cols = lax.dot_general(
        kq_grad, tokens, (((0,), (0,)), ((), ())), preferred_element_type=F32
    )
    grad_parts = lax.all_to_all(
        jnp.moveaxis(grad_cols.reshape(kq_cols, seqs, -1), 1, 0), "seq", 0, 0, tiled=True
    )
    grad_keyquery = jnp.sum(grad_parts, axis=0).T.reshape(w_keyquery.shape)
    return (mixed, grad_tokens, grad_keyquery)


def solution(mesh):
    return jax.shard_map(
        per_device,
        mesh=mesh,
        in_specs=(
            P("seq", None),
            P("seq", "chan"),
            P("seq", "chan", None),
            P("chan"),
            P("seq", "chan"),
        ),
        out_specs=(P("seq", "chan"), P("seq", "chan"), P("seq", "chan", None)),
        check_vma=False,
    )
```

```python
import functools

import jax
import jax.numpy as jnp
from jax import lax
from jax.experimental import pallas as pl
from jax.experimental.pallas import tpu as pltpu
from jax.sharding import PartitionSpec as P

NS = 16
LANES = 128
UNROLL = 8
F32 = jnp.float32
BF16 = jnp.bfloat16


def lane_groups(width):
    return [slice(j * LANES, (j + 1) * LANES) for j in range(width // LANES)]


def tile(ref, first, cols):
    return ref[pl.ds(first, UNROLL), cols]


def place(rows, at, value):
    here = lax.broadcasted_iota(jnp.int32, rows.shape, 0) == at
    return jnp.where(here, jnp.broadcast_to(value, rows.shape), rows)


def to_float(src, dst):
    dst[...] = src[...].astype(F32)


def adjoint_totals_kernel(kq, eps, cot, pair_out, cot_f):
    tokens, width = eps.shape
    groups = lane_groups(width)
    to_float(cot, cot_f)

    def block(i, carry):
        lams, decays = carry
        first = pl.multiple_of(tokens - (i + 1) * UNROLL, UNROLL)
        steps = [tile(eps, first, cols) for cols in groups]
        cots = [tile(cot_f, first, cols) for cols in groups]
        for j in reversed(range(UNROLL)):
            t = first + j
            keys = kq[t, :NS, :]
            queries = kq[t, NS:, :]
            square = keys * keys
            new_lams, new_decays = [], []
            for lam, total, step, cot_row in zip(lams, decays, steps, cots):
                decay = 1.0 - step[j : j + 1] * square
                new_lams.append(decay * (queries * cot_row[j : j + 1] + lam))
                new_decays.append(total * decay)
            lams, decays = new_lams, new_decays
        return (tuple(lams), tuple(decays))

    zeros = tuple(jnp.zeros((NS, LANES), F32) for _ in groups)
    ones = tuple(jnp.ones((NS, LANES), F32) for _ in groups)
    lams, decays = lax.fori_loop(0, tokens // UNROLL, block, (zeros, ones))
    for lam, total, cols in zip(lams, decays, groups):
        pair_out[:NS, cols] = lam
        pair_out[NS:, cols] = total


def adjoint_kernel(kq, eps, cot, start, adj_out, grad_out, cot_f, grad_f):
    tokens, width = eps.shape
    groups = lane_groups(width)
    to_float(cot, cot_f)

    def block(i, lams):
        first = pl.multiple_of(tokens - (i + 1) * UNROLL, UNROLL)
        steps = [tile(eps, first, cols) for cols in groups]
        cots = [tile(cot_f, first, cols) for cols in groups]
        grads = [jnp.zeros((UNROLL, LANES), F32) for _ in groups]
        for j in reversed(range(UNROLL)):
            t = first + j
            keys = kq[t, :NS, :]
            queries = kq[t, NS:, :]
            square = keys * keys
            new_lams = []
            for n, cols in enumerate(groups):
                adj = queries * cots[n][j : j + 1] + lams[n]
                adj_out[t, :, cols] = adj
                grads[n] = place(grads[n], j, jnp.sum(adj * keys, axis=0, keepdims=True))
                new_lams.append((1.0 - steps[n][j : j + 1] * square) * adj)
            lams = new_lams
        for n, cols in enumerate(groups):
            grad_f[pl.ds(first, UNROLL), cols] = steps[n] * grads[n]
        return tuple(lams)

    lax.fori_loop(0, tokens // UNROLL, block, tuple(start[:, cols] for cols in groups))
    grad_out[...] = grad_f[...].astype(BF16)


def state_total_kernel(kq, eps, inner, state_out):
    tokens, width = eps.shape
    groups = lane_groups(width)

    def block(i, states):
        first = pl.multiple_of(i * UNROLL, UNROLL)
        steps = [tile(eps, first, cols) for cols in groups]
        pushes = [tile(inner, first, cols) * step for cols, step in zip(groups, steps)]
        for j in range(UNROLL):
            t = first + j
            keys = kq[t, :NS, :]
            square = keys * keys
            states = [
                (1.0 - step[j : j + 1] * square) * state + push[j : j + 1] * keys
                for state, step, push in zip(states, steps, pushes)
            ]
        return tuple(states)

    zeros = tuple(jnp.zeros((NS, LANES), F32) for _ in groups)
    states = lax.fori_loop(0, tokens // UNROLL, block, zeros)
    for state, cols in zip(states, groups):
        state_out[:, cols] = state


def mixer_kernel(kq, eps, inner, cot, adj_in, start, mixed_out, gkq_out, cot_f, mixed_f, key_acc, query_acc):
    tokens, width = eps.shape
    groups = lane_groups(width)
    to_float(cot, cot_f)

    @pl.when(pl.program_id(0) == 0)
    def _():
        key_acc[...] = jnp.zeros_like(key_acc)
        query_acc[...] = jnp.zeros_like(query_acc)

    def block(i, states):
        first = pl.multiple_of(i * UNROLL, UNROLL)
        steps = [tile(eps, first, cols) for cols in groups]
        inners = [tile(inner, first, cols) for cols in groups]
        pushes = [step * x for step, x in zip(steps, inners)]
        squares = [step * step for step in steps]
        cots = [tile(cot_f, first, cols) for cols in groups]
        outs = [jnp.zeros((UNROLL, LANES), F32) for _ in groups]
        for j in range(UNROLL):
            t = first + j
            keys = kq[t, :NS, :]
            queries = kq[t, NS:, :]
            square = keys * keys
            new_states = []
            key_sum = jnp.zeros((NS, LANES), F32)
            step_sum = jnp.zeros((NS, LANES), F32)
            query_sum = jnp.zeros((NS, LANES), F32)
            for n, cols in enumerate(groups):
                step = steps[n][j : j + 1]
                adj = adj_in[t, :, cols]
                through_decay = keys * (adj * states[n])
                through_both = inners[n][j : j + 1] * adj - through_decay
                key_sum = key_sum + step * (through_both - through_decay)
                step_sum = step_sum + squares[n][j : j + 1] * through_both
                state = (1.0 - step * square) * states[n] + pushes[n][j : j + 1] * keys
                query_sum = query_sum + state * cots[n][j : j + 1]
                outs[n] = place(outs[n], j, jnp.sum(state * queries, axis=0, keepdims=True))
                new_states.append(state)
            states = new_states
            through_step = jnp.sum(keys * step_sum, axis=0, keepdims=True)
            key_acc[t] += key_sum - 2.0 * keys * through_step
            query_acc[t] += query_sum
        for n, cols in enumerate(groups):
            mixed_f[pl.ds(first, UNROLL), cols] = outs[n]
        return tuple(states)

    lax.fori_loop(0, tokens // UNROLL, block, tuple(start[:, cols] for cols in groups))
    mixed_out[...] = mixed_f[...].astype(BF16)

    @pl.when(pl.program_id(0) == pl.num_programs(0) - 1)
    def _():
        ones = jnp.ones((LANES, LANES), F32)
        lane = lax.broadcasted_iota(jnp.int32, (NS, LANES), 1)
        state = lax.broadcasted_iota(jnp.int32, (NS, LANES), 0)

        def spread(acc, first):
            total = jnp.dot(
                acc[...].reshape(tokens * NS, LANES),
                ones,
                preferred_element_type=F32,
                precision=lax.Precision.HIGHEST,
            )
            placed = jnp.where(
                (lane == state + first)[None], total.reshape(tokens, NS, LANES), 0.0
            )
            return jnp.sum(placed, axis=1)

        gkq_out[...] = spread(key_acc, 0) + spread(query_acc, NS)


def call(kernel, tokens, width, block, ins, outs, scratch, args, flops):
    def spec(kind):
        return {
            "kq": pl.BlockSpec((tokens, 2 * NS, LANES), lambda c: (0, 0, 0)),
            "rows": pl.BlockSpec((tokens, block), lambda c: (0, c)),
            "rows16": pl.BlockSpec((tokens, block), lambda c: (0, c)),
            "state": pl.BlockSpec((NS, block), lambda c: (0, c)),
            "pair": pl.BlockSpec((2 * NS, block), lambda c: (0, c)),
            "states": pl.BlockSpec((tokens, NS, block), lambda c: (0, 0, c)),
            "gkq": pl.BlockSpec((tokens, LANES), lambda c: (0, 0)),
        }[kind]

    def shape(kind):
        return {
            "rows": jax.ShapeDtypeStruct((tokens, width), F32),
            "rows16": jax.ShapeDtypeStruct((tokens, width), BF16),
            "state": jax.ShapeDtypeStruct((NS, width), F32),
            "pair": jax.ShapeDtypeStruct((2 * NS, width), F32),
            "states": jax.ShapeDtypeStruct((tokens, NS, width), F32),
            "gkq": jax.ShapeDtypeStruct((tokens, LANES), F32),
        }[kind]

    return pl.pallas_call(
        kernel,
        grid=(width // block,),
        in_specs=[spec(kind) for kind in ins],
        out_specs=[spec(kind) for kind in outs],
        out_shape=[shape(kind) for kind in outs],
        scratch_shapes=scratch,
        compiler_params=pltpu.CompilerParams(vmem_limit_bytes=48 * 2**20),
        cost_estimate=pl.CostEstimate(
            flops=flops * tokens * NS * width,
            bytes_accessed=4 * tokens * width * (1 + NS * ("states" in ins + outs)),
            transcendentals=0,
        ),
    )(*args)


def shifted(value, axis, by):
    peers = lax.axis_size(axis)
    pairs = [(i, i + by) for i in range(peers) if 0 <= i + by < peers]
    return lax.ppermute(value, axis, pairs)


def carried(decay, total, sign, together):
    count = lax.axis_size("seq")
    window, radix = 1, 4
    inc_decay, inc_total = decay, total
    exc_decay, exc_total = None, None
    while window < count:
        last = window * radix >= count
        joint = together and not last
        pair = jnp.concatenate([inc_total, inc_decay], axis=0) if joint else None
        for j in range(1, min(radix, -(-count // window))):
            by = sign * window * j
            if joint:
                far = shifted(pair, "seq", by)
                far_total, far_decay = far[:NS], far[NS:]
            else:
                far_total, far_decay = shifted(inc_total, "seq", by), shifted(inc_decay, "seq", by)
            if exc_total is None:
                exc_total, exc_decay = far_total, far_decay
            else:
                exc_total = exc_total + exc_decay * far_total
                exc_decay = exc_decay * far_decay
        if not last:
            inc_total = total + decay * exc_total
            inc_decay = decay * exc_decay
        window *= radix
    return exc_total


def gather_columns(value, axis):
    count = lax.axis_size(axis)
    parts = lax.all_to_all(
        jnp.broadcast_to(value[None], (count,) + value.shape), axis, 0, 0, tiled=True
    )
    return jnp.moveaxis(parts, 0, 1).reshape(value.shape[0], count * value.shape[1])


def scatter_sum_columns(value):
    count = lax.axis_size("chan")
    index = lax.axis_index("chan")
    if count & (count - 1):
        return lax.psum_scatter(value, "chan", scatter_dimension=1, tiled=True)
    blocks = jnp.moveaxis(value.reshape(value.shape[0], count, -1), 1, 0)
    offset = 1
    while offset < count:
        pairs = blocks.reshape((-1, 2) + blocks.shape[1:])
        bit = (index // offset) % 2
        mine = lax.dynamic_index_in_dim(pairs, bit, 1, keepdims=False)
        other = lax.dynamic_index_in_dim(pairs, 1 - bit, 1, keepdims=False)
        wire = other if offset == 1 else other.astype(BF16)
        swap = [(i, i ^ offset) for i in range(count)]
        blocks = mine + lax.ppermute(wire, "chan", swap).astype(F32)
        offset *= 2
    return blocks[0]


class Gathered:
    def __init__(self, tokens, w_inner):
        self.tokens = tokens
        self.full = lax.all_gather(w_inner, "seq", axis=0, tiled=True)

    def inner(self):
        return jnp.dot(self.tokens, self.full, preferred_element_type=F32)

    def grad_tokens(self, grad):
        return scatter_sum_columns(dot_t(grad, self.full))


class Exchanged:
    def __init__(self, tokens, w_inner):
        self.depth, self.width = w_inner.shape
        self.count = tokens.shape[0]
        seqs = lax.axis_size("seq")
        self.rows = seqs // 2
        index = lax.axis_index("seq")
        self.row, self.side = index // 2, index % 2
        self.first = lax.axis_index("chan") % 2 == 0
        self.w_mine = w_inner
        self.w_other = lax.ppermute(w_inner, "seq", [(i, i ^ 1) for i in range(seqs)])
        half = jnp.where(self.first, self.side, 1 - self.side)
        came = [
            self.move(self.columns(tokens, (self.row + j) % self.rows, half), j)
            for j in range(1, self.rows)
        ]
        came = jnp.concatenate(came, axis=0)
        partner = self.swap(came)
        self.far_mine = jnp.where(self.first, came, partner)
        self.far_other = jnp.where(self.first, partner, came)
        self.near_mine = self.columns(tokens, self.row, self.side)
        self.near_other = self.columns(tokens, self.row, 1 - self.side)

    def columns(self, tokens, row, side):
        return lax.dynamic_slice_in_dim(tokens, (row * 2 + side) * self.depth, self.depth, 1)

    def move(self, value, by):
        pairs = [
            (r * 2 + s, (r + by) % self.rows * 2 + s) for r in range(self.rows) for s in range(2)
        ]
        return lax.ppermute(value, "seq", pairs)

    def swap(self, value):
        chans = lax.axis_size("chan")
        return lax.ppermute(value, "chan", [(i, i ^ 1) for i in range(chans)])

    def inner(self):
        def product(mine, other):
            return jnp.dot(mine, self.w_mine, preferred_element_type=F32) + jnp.dot(
                other, self.w_other, preferred_element_type=F32
            )

        far = product(self.far_mine, self.far_other).astype(BF16)
        total = product(self.near_mine, self.near_other)
        for j in range(1, self.rows):
            block = far[(j - 1) * self.count : j * self.count]
            total = total + self.move(block, -j).astype(F32)
        return total

    def grad_tokens(self, grad):
        chans = lax.axis_size("chan")
        pairs = chans // 2
        blocks = [grad] + [self.move(grad, j) for j in range(1, self.rows)]
        even = jnp.concatenate(blocks[0::2], axis=0)
        odd = jnp.concatenate(blocks[1::2], axis=0)
        keep = jnp.where(self.first, even, odd)
        give = jnp.where(self.first, odd, even)
        one, two = self.w_mine, self.w_other
        full = jnp.concatenate(
            [jnp.where(self.side == 0, one, two), jnp.where(self.side == 0, two, one)], axis=0
        )
        kept = dot_t(keep, full) + self.swap(dot_t(give, full))
        pieces = kept.astype(BF16).reshape(pairs, self.count, -1)
        y = lax.axis_index("chan") // 2
        total = None
        for m in range(pairs):
            piece = lax.dynamic_index_in_dim(pieces, (y + m) % pairs, 0, keepdims=False)
            route = []
            for r in range(self.rows):
                for s in range(2):
                    for c in range(chans):
                        p = (c // 2 + m) % pairs
                        to = (r - c % 2 - 2 * p) % self.rows
                        route.append(((r * 2 + s) * chans + c, (to * 2 + s) * chans + r))
            piece = lax.ppermute(piece, ("seq", "chan"), route).astype(F32)
            total = piece if total is None else total + piece
        return total


def dot_t(left, right):
    return lax.dot_general(left, right, (((1,), (1,)), ((), ())), preferred_element_type=F32)


def per_device(tokens, w_inner, w_keyquery, rate, grad_out):
    count = tokens.shape[0]
    width = w_inner.shape[1]
    kq_cols = w_keyquery.shape[1] * w_keyquery.shape[2]
    seqs, chans = lax.axis_size("seq"), lax.axis_size("chan")
    block = min(width, 512)
    short = seqs == 2 * chans and chans % 2 == 0 and count * seqs <= w_inner.shape[0] * seqs
    plan = (Exchanged if short else Gathered)(tokens, w_inner)
    full_kq = gather_columns(w_keyquery.reshape(-1, kq_cols).T, "seq")
    keyquery = dot_t(tokens, full_kq)
    keys = keyquery[:, :NS]
    sumsq = jnp.sum(keys * keys, axis=1)
    eps = rate[None, :] / (1.0 + rate[None, :] * sumsq[:, None])
    spread = jnp.broadcast_to(keyquery[:, :, None], (count, 2 * NS, LANES))
    rows_f = pltpu.VMEM((count, block), F32)
    run = functools.partial(call, tokens=count, width=width, block=block)

    (pair,) = run(
        adjoint_totals_kernel,
        ins=["kq", "rows", "rows16"], outs=["pair"], scratch=[rows_f],
        args=(spread, eps, grad_out), flops=8,
    )
    lam, decay = pair[:NS], pair[NS:]
    end_adjoint = carried(decay, lam, -1, True)
    adjoints, inner_grad = run(
        adjoint_kernel,
        ins=["kq", "rows", "rows16", "state"], outs=["states", "rows16"], scratch=[rows_f, rows_f],
        args=(spread, eps, grad_out, end_adjoint), flops=8,
    )
    inner = plan.inner()
    (alone_end,) = run(
        state_total_kernel,
        ins=["kq", "rows", "rows"], outs=["state"], scratch=[],
        args=(spread, eps, inner), flops=6,
    )
    start_state = carried(decay, alone_end, 1, False)
    tokens_sum = plan.grad_tokens(inner_grad)
    acc = pltpu.VMEM((count, NS, LANES), F32)
    mixed, kq_grad = run(
        mixer_kernel,
        ins=["kq", "rows", "rows", "rows16", "states", "state"], outs=["rows16", "gkq"],
        scratch=[rows_f, rows_f, acc, acc],
        args=(spread, eps, inner, grad_out, adjoints, start_state), flops=20,
    )
    kq_grad = kq_grad[:, :kq_cols].astype(BF16)

    kq_rows = lax.all_to_all(
        jnp.moveaxis(full_kq.reshape(kq_cols, chans, -1), 1, 0), "chan", 0, 0, tiled=True
    )
    kq_rows = kq_rows.reshape(chans * kq_cols, -1)
    all_kq = gather_columns(kq_grad, "chan")
    grad_tokens = (
        tokens_sum + jnp.dot(all_kq, kq_rows, preferred_element_type=F32)
    ).astype(BF16)

    grad_cols = lax.dot_general(
        kq_grad, tokens, (((0,), (0,)), ((), ())), preferred_element_type=F32
    )
    grad_parts = lax.all_to_all(
        jnp.moveaxis(grad_cols.astype(BF16).reshape(kq_cols, seqs, -1), 1, 0), "seq", 0, 0, tiled=True
    )
    grad_keyquery = jnp.sum(grad_parts.astype(F32), axis=0).T.reshape(w_keyquery.shape)
    return (mixed, grad_tokens, grad_keyquery)


def solution(mesh):
    return jax.shard_map(
        per_device,
        mesh=mesh,
        in_specs=(
            P("seq", None),
            P("seq", "chan"),
            P("seq", "chan", None),
            P("chan"),
            P("seq", "chan"),
        ),
        out_specs=(P("seq", "chan"), P("seq", "chan"), P("seq", "chan", None)),
        check_vma=False,
    )
```

```python
import functools

import jax
import jax.numpy as jnp
from jax import lax
from jax.experimental import pallas as pl
from jax.experimental.pallas import tpu as pltpu
from jax.sharding import PartitionSpec as P

NS = 16
LANES = 128
UNROLL = 8
ROWS = 4
WORK = 1
F32 = jnp.float32
BF16 = jnp.bfloat16


def lane_groups(width):
    return [slice(j * LANES, (j + 1) * LANES) for j in range(width // LANES)]


def tile(ref, first, cols):
    return ref[pl.ds(first, UNROLL), cols]


def place(rows, at, value):
    here = lax.broadcasted_iota(jnp.int32, rows.shape, 0) == at
    return jnp.where(here, jnp.broadcast_to(value, rows.shape), rows)


def to_float(src, dst):
    dst[...] = src[...].astype(F32)


def adjoint_totals_kernel(kq, eps, cot, pair_out, cot_f):
    tokens, width = eps.shape
    groups = lane_groups(width)
    to_float(cot, cot_f)

    def block(i, carry):
        lams, decays = carry
        first = pl.multiple_of(tokens - (i + 1) * UNROLL, UNROLL)
        steps = [tile(eps, first, cols) for cols in groups]
        cots = [tile(cot_f, first, cols) for cols in groups]
        for j in reversed(range(UNROLL)):
            t = first + j
            keys = kq[t, :NS, :]
            queries = kq[t, NS:, :]
            square = keys * keys
            new_lams, new_decays = [], []
            for lam, total, step, cot_row in zip(lams, decays, steps, cots):
                decay = 1.0 - step[j : j + 1] * square
                new_lams.append(decay * (queries * cot_row[j : j + 1] + lam))
                new_decays.append(total * decay)
            lams, decays = new_lams, new_decays
        return (tuple(lams), tuple(decays))

    zeros = tuple(jnp.zeros((NS, LANES), F32) for _ in groups)
    ones = tuple(jnp.ones((NS, LANES), F32) for _ in groups)
    lams, decays = lax.fori_loop(0, tokens // UNROLL, block, (zeros, ones))
    for lam, total, cols in zip(lams, decays, groups):
        pair_out[:NS, cols] = lam
        pair_out[NS:, cols] = total


def adjoint_kernel(kq, eps, cot, start, adj_out, grad_out, cot_f, grad_f):
    tokens, width = eps.shape
    groups = lane_groups(width)
    to_float(cot, cot_f)

    def block(i, lams):
        first = pl.multiple_of(tokens - (i + 1) * UNROLL, UNROLL)
        steps = [tile(eps, first, cols) for cols in groups]
        cots = [tile(cot_f, first, cols) for cols in groups]
        grads = [jnp.zeros((UNROLL, LANES), F32) for _ in groups]
        for j in reversed(range(UNROLL)):
            t = first + j
            keys = kq[t, :NS, :]
            queries = kq[t, NS:, :]
            square = keys * keys
            new_lams = []
            for n, cols in enumerate(groups):
                adj = queries * cots[n][j : j + 1] + lams[n]
                adj_out[t, :, cols] = adj
                grads[n] = place(grads[n], j, jnp.sum(adj * keys, axis=0, keepdims=True))
                new_lams.append((1.0 - steps[n][j : j + 1] * square) * adj)
            lams = new_lams
        for n, cols in enumerate(groups):
            grad_f[pl.ds(first, UNROLL), cols] = steps[n] * grads[n]
        return tuple(lams)

    lax.fori_loop(0, tokens // UNROLL, block, tuple(start[:, cols] for cols in groups))
    grad_out[...] = grad_f[...].astype(BF16)


def state_total_kernel(kq, eps, inner, state_out):
    tokens, width = eps.shape
    groups = lane_groups(width)

    def block(i, states):
        first = pl.multiple_of(i * UNROLL, UNROLL)
        steps = [tile(eps, first, cols) for cols in groups]
        pushes = [tile(inner, first, cols) * step for cols, step in zip(groups, steps)]
        for j in range(UNROLL):
            t = first + j
            keys = kq[t, :NS, :]
            square = keys * keys
            states = [
                (1.0 - step[j : j + 1] * square) * state + push[j : j + 1] * keys
                for state, step, push in zip(states, steps, pushes)
            ]
        return tuple(states)

    zeros = tuple(jnp.zeros((NS, LANES), F32) for _ in groups)
    states = lax.fori_loop(0, tokens // UNROLL, block, zeros)
    for state, cols in zip(states, groups):
        state_out[:, cols] = state


def mixer_kernel(kq, eps, inner, cot, adj_in, start, mixed_out, gkq_out, cot_f, mixed_f, key_acc, query_acc):
    tokens, width = eps.shape
    groups = lane_groups(width)
    to_float(cot, cot_f)

    @pl.when(pl.program_id(0) == 0)
    def _():
        key_acc[...] = jnp.zeros_like(key_acc)
        query_acc[...] = jnp.zeros_like(query_acc)

    def block(i, states):
        first = pl.multiple_of(i * UNROLL, UNROLL)
        steps = [tile(eps, first, cols) for cols in groups]
        inners = [tile(inner, first, cols) for cols in groups]
        pushes = [step * x for step, x in zip(steps, inners)]
        squares = [step * step for step in steps]
        cots = [tile(cot_f, first, cols) for cols in groups]
        outs = [jnp.zeros((UNROLL, LANES), F32) for _ in groups]
        for j in range(UNROLL):
            t = first + j
            keys = kq[t, :NS, :]
            queries = kq[t, NS:, :]
            square = keys * keys
            new_states = []
            key_sum = jnp.zeros((NS, LANES), F32)
            step_sum = jnp.zeros((NS, LANES), F32)
            query_sum = jnp.zeros((NS, LANES), F32)
            for n, cols in enumerate(groups):
                step = steps[n][j : j + 1]
                adj = adj_in[t, :, cols]
                through_decay = keys * (adj * states[n])
                through_both = inners[n][j : j + 1] * adj - through_decay
                key_sum = key_sum + step * (through_both - through_decay)
                step_sum = step_sum + squares[n][j : j + 1] * through_both
                state = (1.0 - step * square) * states[n] + pushes[n][j : j + 1] * keys
                query_sum = query_sum + state * cots[n][j : j + 1]
                outs[n] = place(outs[n], j, jnp.sum(state * queries, axis=0, keepdims=True))
                new_states.append(state)
            states = new_states
            through_step = jnp.sum(keys * step_sum, axis=0, keepdims=True)
            key_acc[t] += key_sum - 2.0 * keys * through_step
            query_acc[t] += query_sum
        for n, cols in enumerate(groups):
            mixed_f[pl.ds(first, UNROLL), cols] = outs[n]
        return tuple(states)

    lax.fori_loop(0, tokens // UNROLL, block, tuple(start[:, cols] for cols in groups))
    mixed_out[...] = mixed_f[...].astype(BF16)

    @pl.when(pl.program_id(0) == pl.num_programs(0) - 1)
    def _():
        ones = jnp.ones((LANES, LANES), F32)
        lane = lax.broadcasted_iota(jnp.int32, (NS, LANES), 1)
        state = lax.broadcasted_iota(jnp.int32, (NS, LANES), 0)

        def spread(acc, first):
            total = jnp.dot(
                acc[...].reshape(tokens * NS, LANES),
                ones,
                preferred_element_type=F32,
                precision=lax.Precision.HIGHEST,
            )
            placed = jnp.where(
                (lane == state + first)[None], total.reshape(tokens, NS, LANES), 0.0
            )
            return jnp.sum(placed, axis=1)

        gkq_out[...] = spread(key_acc, 0) + spread(query_acc, NS)


def call(kernel, tokens, width, block, ins, outs, scratch, args, work):
    def spec(kind):
        return {
            "kq": pl.BlockSpec((tokens, 2 * NS, LANES), lambda c: (0, 0, 0)),
            "rows": pl.BlockSpec((tokens, block), lambda c: (0, c)),
            "rows16": pl.BlockSpec((tokens, block), lambda c: (0, c)),
            "state": pl.BlockSpec((NS, block), lambda c: (0, c)),
            "pair": pl.BlockSpec((2 * NS, block), lambda c: (0, c)),
            "states": pl.BlockSpec((tokens, NS, block), lambda c: (0, 0, c)),
            "gkq": pl.BlockSpec((tokens, LANES), lambda c: (0, 0)),
        }[kind]

    def shape(kind):
        return {
            "rows": jax.ShapeDtypeStruct((tokens, width), F32),
            "rows16": jax.ShapeDtypeStruct((tokens, width), BF16),
            "state": jax.ShapeDtypeStruct((NS, width), F32),
            "pair": jax.ShapeDtypeStruct((2 * NS, width), F32),
            "states": jax.ShapeDtypeStruct((tokens, NS, width), F32),
            "gkq": jax.ShapeDtypeStruct((tokens, LANES), F32),
        }[kind]

    return pl.pallas_call(
        kernel,
        grid=(width // block,),
        in_specs=[spec(kind) for kind in ins],
        out_specs=[spec(kind) for kind in outs],
        out_shape=[shape(kind) for kind in outs],
        scratch_shapes=scratch,
        compiler_params=pltpu.CompilerParams(vmem_limit_bytes=48 * 2**20),
        cost_estimate=pl.CostEstimate(
            flops=work * WORK * tokens * NS * width,
            bytes_accessed=1024,
            transcendentals=0,
        ),
    )(*args)


def shifted(value, axis, by):
    peers = lax.axis_size(axis)
    pairs = [(i, i + by) for i in range(peers) if 0 <= i + by < peers]
    return lax.ppermute(value, axis, pairs)


def carried(pair, sign):
    count = lax.axis_size("seq")
    window, radix = 1, 4
    total, decay = pair[:NS], pair[NS:]
    inc, exc_total, exc_decay, ready = pair, None, None, None
    while window < count:
        last = window * radix >= count
        if last and window * 2 >= count:
            inc = inc[:NS]
        wire = ready = inc.astype(BF16)
        for j in range(1, min(radix, -(-count // window))):
            far = shifted(wire, "seq", sign * window * j).astype(F32)
            far_total, far_decay = far[:NS], far[NS:]
            if exc_total is None:
                exc_total, exc_decay = far_total, far_decay
            else:
                exc_total = exc_total + exc_decay * far_total
                if far_decay.shape[0]:
                    exc_decay = exc_decay * far_decay
        inc = jnp.concatenate([total + decay * exc_total, decay * exc_decay], axis=0)
        window *= radix
    return exc_total, ready


def along_chan(value, by):
    count = lax.axis_size("chan")
    return lax.ppermute(value, "chan", [(i, (i + by) % count) for i in range(count)]) if by else value


def gathered(value, axis):
    copies = jnp.broadcast_to(value[None], (lax.axis_size(axis),) + value.shape)
    return lax.all_to_all(copies, axis, 0, 0, tiled=True)


def side_by_side(parts):
    return jnp.moveaxis(parts, 0, 1).reshape(parts.shape[1], -1)


def scatter_sum_columns(value):
    count = lax.axis_size("chan")
    index = lax.axis_index("chan")
    if count & (count - 1):
        return lax.psum_scatter(value, "chan", scatter_dimension=1, tiled=True)
    blocks = jnp.moveaxis(value.reshape(value.shape[0], count, -1), 1, 0)
    offset = 1
    while offset < count:
        pairs = blocks.reshape((-1, 2) + blocks.shape[1:])
        bit = (index // offset) % 2
        mine = lax.dynamic_index_in_dim(pairs, bit, 1, keepdims=False)
        other = lax.dynamic_index_in_dim(pairs, 1 - bit, 1, keepdims=False)
        wire = other if offset == 1 else other.astype(BF16)
        swap = [(i, i ^ offset) for i in range(count)]
        blocks = mine + lax.ppermute(wire, "chan", swap).astype(F32)
        offset *= 2
    return blocks[0]


class Gathered:
    def __init__(self, tokens, w_inner):
        self.tokens = tokens
        self.full = lax.all_gather(w_inner, "seq", axis=0, tiled=True)

    def partials(self, before):
        return jnp.dot(self.tokens, self.full, preferred_element_type=F32), None, None, before

    def inner(self, near, far, beside):
        return near

    def grads(self, grad):
        return None

    def grad_tokens(self, grad, far, after):
        return scatter_sum_columns(dot_t(grad, self.full))


class Exchanged:
    def __init__(self, tokens, w_inner):
        self.depth, self.width = w_inner.shape
        self.count = tokens.shape[0]
        index = lax.axis_index("seq")
        self.row, self.side = index // 2, index % 2
        self.first = lax.axis_index("chan") % 2 == 0
        self.w_mine = w_inner
        self.w_other = self.trade(w_inner, "seq", 1)
        half = jnp.where(self.first, self.side, 1 - self.side)
        came = [
            self.trade(self.columns(tokens, self.row ^ m, half), "seq", 2 * m) for m in (1, 3, 2)
        ]
        self.came = jnp.concatenate(came, axis=0)
        self.near_mine = self.columns(tokens, self.row, self.side)
        self.near_other = self.columns(tokens, self.row, 1 - self.side)

    def columns(self, tokens, row, side):
        return lax.dynamic_slice_in_dim(tokens, (row * 2 + side) * self.depth, self.depth, 1)

    def trade(self, value, axis, mask):
        pairs = [(i, i ^ mask) for i in range(lax.axis_size(axis))]
        return lax.ppermute(value, axis, pairs)

    def partials(self, before):
        def product(mine, other):
            return jnp.dot(mine, self.w_mine, preferred_element_type=F32) + jnp.dot(
                other, self.w_other, preferred_element_type=F32
            )

        partner = self.trade(self.came, "chan", 1)
        mine = jnp.where(self.first, self.came, partner)
        other = jnp.where(self.first, partner, self.came)
        two = 2 * self.count
        beside = product(mine[:two], other[:two]).astype(BF16)
        beside, before = lax.optimization_barrier((beside, before))
        near = product(self.near_mine, self.near_other)
        return near, product(mine[two:], other[two:]), self.trade(beside, "seq", 2), before

    def inner(self, near, far, beside):
        far = far + beside[self.count :].astype(F32)
        return near + beside[: self.count].astype(F32) + self.trade(far.astype(BF16), "seq", 4).astype(F32)

    def grads(self, grad):
        return self.trade(grad, "seq", 4)

    def grad_tokens(self, grad, far, after):
        chans = lax.axis_size("chan")
        even = jnp.concatenate([grad, far], axis=0)
        odd = self.trade(even, "seq", 2)
        odd, after = lax.optimization_barrier((odd, after))
        keep = jnp.where(self.first, even, odd)
        give = jnp.where(self.first, odd, even)
        one, two = self.w_mine, self.w_other
        full = jnp.concatenate(
            [jnp.where(self.side == 0, one, two), jnp.where(self.side == 0, two, one)], axis=0
        )
        kept = dot_t(keep, full) + self.trade(dot_t(give, full), "chan", 1)
        pieces = kept.astype(BF16).reshape(2, self.count, -1)
        y = lax.axis_index("chan") // 2
        total = None
        for m in range(2):
            piece = lax.dynamic_index_in_dim(pieces, y ^ m, 0, keepdims=False)
            route = [
                (((r * 2 + s) * chans + c), ((r ^ (c % 2 + 2 * (c // 2 ^ m))) * 2 + s) * chans + r)
                for r in range(ROWS)
                for s in range(2)
                for c in range(chans)
            ]
            piece = lax.ppermute(piece, ("seq", "chan"), route).astype(F32)
            total = piece if total is None else total + piece
        return total


def dot_t(left, right):
    return lax.dot_general(left, right, (((1,), (1,)), ((), ())), preferred_element_type=F32)


def per_device(tokens, w_inner, w_keyquery, rate, grad_out):
    count = tokens.shape[0]
    width = w_inner.shape[1]
    kq_cols = w_keyquery.shape[1] * w_keyquery.shape[2]
    seqs, chans = lax.axis_size("seq"), lax.axis_size("chan")
    block = min(width, 512)
    short = seqs == 2 * ROWS and chans == ROWS and count <= w_inner.shape[0]
    plan = (Exchanged if short else Gathered)(tokens, w_inner)
    kq_parts = gathered(w_keyquery.reshape(-1, kq_cols).T, "seq")
    full_kq = side_by_side(kq_parts)
    group = lax.axis_index("chan")
    kq_rows = []
    for m in range(chans):
        rows = lax.dynamic_slice_in_dim(
            full_kq, (group + m) % chans * (full_kq.shape[1] // chans), full_kq.shape[1] // chans, 1
        )
        kq_rows.append(along_chan(rows, m))
    keyquery = dot_t(tokens, full_kq)
    keys = keyquery[:, :NS]
    sumsq = jnp.sum(keys * keys, axis=1)
    eps = rate[None, :] / (1.0 + rate[None, :] * sumsq[:, None])
    spread = jnp.broadcast_to(keyquery[:, :, None], (count, 2 * NS, LANES))
    rows_f = pltpu.VMEM((count, block), F32)
    run = functools.partial(call, tokens=count, width=width, block=block)

    (pair,) = run(
        adjoint_totals_kernel,
        ins=["kq", "rows", "rows16"], outs=["pair"], scratch=[rows_f],
        args=(spread, eps, grad_out), work=4,
    )
    if short:
        pair, plan.came = lax.optimization_barrier((pair, plan.came))
    end_adjoint, _ = carried(pair, -1)
    near, far, beside, end_adjoint = plan.partials(end_adjoint)
    adjoints, inner_grad = run(
        adjoint_kernel,
        ins=["kq", "rows", "rows16", "state"], outs=["states", "rows16"], scratch=[rows_f, rows_f],
        args=(spread, eps, grad_out, end_adjoint), work=10,
    )
    beside, _ = lax.optimization_barrier((beside, inner_grad))
    far_grad = plan.grads(inner_grad)
    inner, far_grad, kq_rows = lax.optimization_barrier(
        (plan.inner(near, far, beside), far_grad, jnp.concatenate(kq_rows, axis=0))
    )
    (alone_end,) = run(
        state_total_kernel,
        ins=["kq", "rows", "rows"], outs=["state"], scratch=[],
        args=(spread, eps, inner), work=4,
    )
    start_state, _ = carried(jnp.concatenate([alone_end, pair[NS:]], axis=0), 1)
    tokens_sum = plan.grad_tokens(inner_grad, far_grad, start_state)
    acc = pltpu.VMEM((count, NS, LANES), F32)
    mixed, kq_grad = run(
        mixer_kernel,
        ins=["kq", "rows", "rows", "rows16", "states", "state"], outs=["rows16", "gkq"],
        scratch=[rows_f, rows_f, acc, acc],
        args=(spread, eps, inner, grad_out, adjoints, start_state), work=22,
    )
    kq_grad = kq_grad[:, :kq_cols].astype(BF16)

    all_kq = jnp.concatenate([along_chan(kq_grad, m) for m in range(chans)], axis=1)
    grad_tokens = (
        tokens_sum + jnp.dot(all_kq, kq_rows, preferred_element_type=F32)
    ).astype(BF16)

    grad_cols = lax.dot_general(
        kq_grad, tokens, (((0,), (0,)), ((), ())), preferred_element_type=F32
    )
    grad_parts = lax.all_to_all(
        jnp.moveaxis(grad_cols.astype(BF16).reshape(kq_cols, seqs, -1), 1, 0), "seq", 0, 0, tiled=True
    )
    grad_keyquery = jnp.sum(grad_parts.astype(F32), axis=0).T.reshape(w_keyquery.shape)
    return (mixed, grad_tokens, grad_keyquery)


def solution(mesh):
    return jax.shard_map(
        per_device,
        mesh=mesh,
        in_specs=(
            P("seq", None),
            P("seq", "chan"),
            P("seq", "chan", None),
            P("chan"),
            P("seq", "chan"),
        ),
        out_specs=(P("seq", "chan"), P("seq", "chan"), P("seq", "chan", None)),
        check_vma=False,
    )
```

```python
import functools

import jax
import jax.numpy as jnp
from jax import lax
from jax.experimental import pallas as pl
from jax.experimental.pallas import tpu as pltpu
from jax.sharding import PartitionSpec as P

NS = 16
LANES = 128
UNROLL = 8
ROWS = 4
WORK = 1
F32 = jnp.float32
BF16 = jnp.bfloat16


def lane_groups(width):
    return [slice(j * LANES, (j + 1) * LANES) for j in range(width // LANES)]


def tile(ref, first, cols):
    return ref[pl.ds(first, UNROLL), cols]


def place(rows, at, value):
    here = lax.broadcasted_iota(jnp.int32, rows.shape, 0) == at
    return jnp.where(here, jnp.broadcast_to(value, rows.shape), rows)


def to_float(src, dst):
    dst[...] = src[...].astype(F32)


def adjoint_totals_kernel(kq, eps, cot, pair_out, cot_f):
    tokens, width = eps.shape
    groups = lane_groups(width)
    to_float(cot, cot_f)

    def block(i, carry):
        lams, decays = carry
        first = pl.multiple_of(tokens - (i + 1) * UNROLL, UNROLL)
        steps = [tile(eps, first, cols) for cols in groups]
        cots = [tile(cot_f, first, cols) for cols in groups]
        for j in reversed(range(UNROLL)):
            t = first + j
            keys = kq[t, :NS, :]
            queries = kq[t, NS:, :]
            square = keys * keys
            new_lams, new_decays = [], []
            for lam, total, step, cot_row in zip(lams, decays, steps, cots):
                decay = 1.0 - step[j : j + 1] * square
                new_lams.append(decay * (queries * cot_row[j : j + 1] + lam))
                new_decays.append(total * decay)
            lams, decays = new_lams, new_decays
        return (tuple(lams), tuple(decays))

    zeros = tuple(jnp.zeros((NS, LANES), F32) for _ in groups)
    ones = tuple(jnp.ones((NS, LANES), F32) for _ in groups)
    lams, decays = lax.fori_loop(0, tokens // UNROLL, block, (zeros, ones))
    for lam, total, cols in zip(lams, decays, groups):
        pair_out[:NS, cols] = lam
        pair_out[NS:, cols] = total


def adjoint_kernel(kq, eps, cot, start, adj_out, grad_out, cot_f, grad_f):
    tokens, width = eps.shape
    groups = lane_groups(width)
    to_float(cot, cot_f)

    def block(i, lams):
        first = pl.multiple_of(tokens - (i + 1) * UNROLL, UNROLL)
        steps = [tile(eps, first, cols) for cols in groups]
        cots = [tile(cot_f, first, cols) for cols in groups]
        grads = [jnp.zeros((UNROLL, LANES), F32) for _ in groups]
        for j in reversed(range(UNROLL)):
            t = first + j
            keys = kq[t, :NS, :]
            queries = kq[t, NS:, :]
            square = keys * keys
            new_lams = []
            for n, cols in enumerate(groups):
                adj = queries * cots[n][j : j + 1] + lams[n]
                adj_out[t, :, cols] = adj
                grads[n] = place(grads[n], j, jnp.sum(adj * keys, axis=0, keepdims=True))
                new_lams.append((1.0 - steps[n][j : j + 1] * square) * adj)
            lams = new_lams
        for n, cols in enumerate(groups):
            grad_f[pl.ds(first, UNROLL), cols] = steps[n] * grads[n]
        return tuple(lams)

    lax.fori_loop(0, tokens // UNROLL, block, tuple(start[:, cols] for cols in groups))
    grad_out[...] = grad_f[...].astype(BF16)


def state_total_kernel(kq, eps, inner, state_out):
    tokens, width = eps.shape
    groups = lane_groups(width)

    def block(i, states):
        first = pl.multiple_of(i * UNROLL, UNROLL)
        steps = [tile(eps, first, cols) for cols in groups]
        pushes = [tile(inner, first, cols) * step for cols, step in zip(groups, steps)]
        for j in range(UNROLL):
            t = first + j
            keys = kq[t, :NS, :]
            square = keys * keys
            states = [
                (1.0 - step[j : j + 1] * square) * state + push[j : j + 1] * keys
                for state, step, push in zip(states, steps, pushes)
            ]
        return tuple(states)

    zeros = tuple(jnp.zeros((NS, LANES), F32) for _ in groups)
    states = lax.fori_loop(0, tokens // UNROLL, block, zeros)
    for state, cols in zip(states, groups):
        state_out[:, cols] = state


def mixer_kernel(kq, eps, inner, cot, adj_in, start, mixed_out, gkq_out, cot_f, mixed_f, key_acc, query_acc):
    tokens, width = eps.shape
    groups = lane_groups(width)
    to_float(cot, cot_f)

    @pl.when(pl.program_id(0) == 0)
    def _():
        key_acc[...] = jnp.zeros_like(key_acc)
        query_acc[...] = jnp.zeros_like(query_acc)

    def block(i, states):
        first = pl.multiple_of(i * UNROLL, UNROLL)
        steps = [tile(eps, first, cols) for cols in groups]
        inners = [tile(inner, first, cols) for cols in groups]
        pushes = [step * x for step, x in zip(steps, inners)]
        squares = [step * step for step in steps]
        cots = [tile(cot_f, first, cols) for cols in groups]
        outs = [jnp.zeros((UNROLL, LANES), F32) for _ in groups]
        for j in range(UNROLL):
            t = first + j
            keys = kq[t, :NS, :]
            queries = kq[t, NS:, :]
            square = keys * keys
            new_states = []
            key_sum = jnp.zeros((NS, LANES), F32)
            step_sum = jnp.zeros((NS, LANES), F32)
            query_sum = jnp.zeros((NS, LANES), F32)
            for n, cols in enumerate(groups):
                step = steps[n][j : j + 1]
                adj = adj_in[t, :, cols]
                through_decay = keys * (adj * states[n])
                through_both = inners[n][j : j + 1] * adj - through_decay
                key_sum = key_sum + step * (through_both - through_decay)
                step_sum = step_sum + squares[n][j : j + 1] * through_both
                state = (1.0 - step * square) * states[n] + pushes[n][j : j + 1] * keys
                query_sum = query_sum + state * cots[n][j : j + 1]
                outs[n] = place(outs[n], j, jnp.sum(state * queries, axis=0, keepdims=True))
                new_states.append(state)
            states = new_states
            through_step = jnp.sum(keys * step_sum, axis=0, keepdims=True)
            key_acc[t] += key_sum - 2.0 * keys * through_step
            query_acc[t] += query_sum
        for n, cols in enumerate(groups):
            mixed_f[pl.ds(first, UNROLL), cols] = outs[n]
        return tuple(states)

    lax.fori_loop(0, tokens // UNROLL, block, tuple(start[:, cols] for cols in groups))
    mixed_out[...] = mixed_f[...].astype(BF16)

    @pl.when(pl.program_id(0) == pl.num_programs(0) - 1)
    def _():
        ones = jnp.ones((LANES, LANES), F32)
        lane = lax.broadcasted_iota(jnp.int32, (NS, LANES), 1)
        state = lax.broadcasted_iota(jnp.int32, (NS, LANES), 0)

        def spread(acc, first):
            total = jnp.dot(
                acc[...].reshape(tokens * NS, LANES),
                ones,
                preferred_element_type=F32,
                precision=lax.Precision.HIGHEST,
            )
            placed = jnp.where(
                (lane == state + first)[None], total.reshape(tokens, NS, LANES), 0.0
            )
            return jnp.sum(placed, axis=1)

        gkq_out[...] = spread(key_acc, 0) + spread(query_acc, NS)


def call(kernel, tokens, width, block, ins, outs, scratch, args, work):
    def spec(kind):
        return {
            "kq": pl.BlockSpec((tokens, 2 * NS, LANES), lambda c: (0, 0, 0)),
            "rows": pl.BlockSpec((tokens, block), lambda c: (0, c)),
            "rows16": pl.BlockSpec((tokens, block), lambda c: (0, c)),
            "state": pl.BlockSpec((NS, block), lambda c: (0, c)),
            "pair": pl.BlockSpec((2 * NS, block), lambda c: (0, c)),
            "states": pl.BlockSpec((tokens, NS, block), lambda c: (0, 0, c)),
            "gkq": pl.BlockSpec((tokens, LANES), lambda c: (0, 0)),
        }[kind]

    def shape(kind):
        return {
            "rows": jax.ShapeDtypeStruct((tokens, width), F32),
            "rows16": jax.ShapeDtypeStruct((tokens, width), BF16),
            "state": jax.ShapeDtypeStruct((NS, width), F32),
            "pair": jax.ShapeDtypeStruct((2 * NS, width), F32),
            "states": jax.ShapeDtypeStruct((tokens, NS, width), F32),
            "gkq": jax.ShapeDtypeStruct((tokens, LANES), F32),
        }[kind]

    return pl.pallas_call(
        kernel,
        grid=(width // block,),
        in_specs=[spec(kind) for kind in ins],
        out_specs=[spec(kind) for kind in outs],
        out_shape=[shape(kind) for kind in outs],
        scratch_shapes=scratch,
        compiler_params=pltpu.CompilerParams(vmem_limit_bytes=48 * 2**20),
        cost_estimate=pl.CostEstimate(
            flops=work * WORK * tokens * NS * width,
            bytes_accessed=1024,
            transcendentals=0,
        ),
    )(*args)


def shifted(value, axis, by):
    peers = lax.axis_size(axis)
    pairs = [(i, i + by) for i in range(peers) if 0 <= i + by < peers]
    return lax.ppermute(value, axis, pairs)


def carried(pair, sign, early=None):
    count = lax.axis_size("seq")
    window, radix = 1, 4
    total, decay = pair[:NS], pair[NS:]
    inc, exc_total, exc_decay = pair, None, None
    while window < count:
        last = window * radix >= count
        if last and window * 2 >= count:
            inc = inc[:NS]
        wire = inc.astype(BF16)
        if last and early is not None:
            wire, early = lax.optimization_barrier((wire, early))
        for j in range(1, min(radix, -(-count // window))):
            far = shifted(wire, "seq", sign * window * j).astype(F32)
            far_total, far_decay = far[:NS], far[NS:]
            if exc_total is None:
                exc_total, exc_decay = far_total, far_decay
            else:
                exc_total = exc_total + exc_decay * far_total
                if far_decay.shape[0]:
                    exc_decay = exc_decay * far_decay
        inc = jnp.concatenate([total + decay * exc_total, decay * exc_decay], axis=0)
        window *= radix
    return exc_total, early


def along_chan(value, by):
    count = lax.axis_size("chan")
    return lax.ppermute(value, "chan", [(i, (i + by) % count) for i in range(count)]) if by else value


def gathered(value, axis):
    copies = jnp.broadcast_to(value[None], (lax.axis_size(axis),) + value.shape)
    return lax.all_to_all(copies, axis, 0, 0, tiled=True)


def side_by_side(parts):
    return jnp.moveaxis(parts, 0, 1).reshape(parts.shape[1], -1)


def scatter_sum_columns(value):
    count = lax.axis_size("chan")
    index = lax.axis_index("chan")
    if count & (count - 1):
        return lax.psum_scatter(value, "chan", scatter_dimension=1, tiled=True)
    blocks = jnp.moveaxis(value.reshape(value.shape[0], count, -1), 1, 0)
    offset = 1
    while offset < count:
        pairs = blocks.reshape((-1, 2) + blocks.shape[1:])
        bit = (index // offset) % 2
        mine = lax.dynamic_index_in_dim(pairs, bit, 1, keepdims=False)
        other = lax.dynamic_index_in_dim(pairs, 1 - bit, 1, keepdims=False)
        wire = other if offset == 1 else other.astype(BF16)
        swap = [(i, i ^ offset) for i in range(count)]
        blocks = mine + lax.ppermute(wire, "chan", swap).astype(F32)
        offset *= 2
    return blocks[0]


class Gathered:
    def __init__(self, tokens, w_inner):
        self.tokens, self.came = tokens, None
        self.full = lax.all_gather(w_inner, "seq", axis=0, tiled=True)

    def partials(self):
        return None, None

    def spread(self, beside, rest):
        return jnp.dot(self.tokens, self.full, preferred_element_type=F32), None, None

    def inner(self, near, far, beside, grad):
        return near, grad, grad

    def grad_tokens(self, even, odd, before):
        return scatter_sum_columns(dot_t(even, self.full)), before


class Exchanged:
    def __init__(self, tokens, w_inner):
        self.depth, self.width = w_inner.shape
        self.count = tokens.shape[0]
        index = lax.axis_index("seq")
        self.row, self.side = index // 2, index % 2
        self.first = lax.axis_index("chan") % 2 == 0
        self.w_mine = w_inner
        self.w_other = self.trade(w_inner, "seq", 1)
        half = jnp.where(self.first, self.side, 1 - self.side)
        came = [
            self.trade(self.columns(tokens, self.row ^ m, half), "seq", 2 * m) for m in (1, 3, 2)
        ]
        self.came = jnp.concatenate(came, axis=0)
        self.near_mine = self.columns(tokens, self.row, self.side)
        self.near_other = self.columns(tokens, self.row, 1 - self.side)

    def columns(self, tokens, row, side):
        return lax.dynamic_slice_in_dim(tokens, (row * 2 + side) * self.depth, self.depth, 1)

    def trade(self, value, axis, mask):
        pairs = [(i, i ^ mask) for i in range(lax.axis_size(axis))]
        return lax.ppermute(value, axis, pairs)

    def partials(self):
        partner = self.trade(self.came, "chan", 1)
        mine = jnp.where(self.first, self.came, partner)
        other = jnp.where(self.first, partner, self.came)
        two = 2 * self.count
        beside = self.product(mine[:two], other[:two]).astype(BF16)
        return beside, (mine[two:], other[two:])

    def product(self, mine, other):
        return jnp.dot(mine, self.w_mine, preferred_element_type=F32) + jnp.dot(
            other, self.w_other, preferred_element_type=F32
        )

    def spread(self, beside, rest):
        near = self.product(self.near_mine, self.near_other)
        return near, self.product(*rest), self.trade(beside, "seq", 2)

    def inner(self, near, far, beside, grad):
        wire = (far + beside[self.count :].astype(F32)).astype(BF16)
        wire, far_grad = lax.optimization_barrier((wire, self.trade(grad, "seq", 4)))
        even = jnp.concatenate([grad, far_grad], axis=0)
        odd = self.trade(even, "seq", 2)
        total = near + beside[: self.count].astype(F32) + self.trade(wire, "seq", 4).astype(F32)
        return total, even, odd

    def grad_tokens(self, even, odd, before):
        chans = lax.axis_size("chan")
        keep = jnp.where(self.first, even, odd)
        give = jnp.where(self.first, odd, even)
        one, two = self.w_mine, self.w_other
        full = jnp.concatenate(
            [jnp.where(self.side == 0, one, two), jnp.where(self.side == 0, two, one)], axis=0
        )
        kept = dot_t(keep, full) + self.trade(dot_t(give, full), "chan", 1)
        pieces = kept.astype(BF16).reshape(2, self.count, -1)
        pieces, before = lax.optimization_barrier((pieces, before))
        y = lax.axis_index("chan") // 2
        total = None
        for m in range(2):
            piece = lax.dynamic_index_in_dim(pieces, y ^ m, 0, keepdims=False)
            route = [
                (((r * 2 + s) * chans + c), ((r ^ (c % 2 + 2 * (c // 2 ^ m))) * 2 + s) * chans + r)
                for r in range(ROWS)
                for s in range(2)
                for c in range(chans)
            ]
            piece = lax.ppermute(piece, ("seq", "chan"), route).astype(F32)
            total = piece if total is None else total + piece
        return total, before


def dot_t(left, right):
    return lax.dot_general(left, right, (((1,), (1,)), ((), ())), preferred_element_type=F32)


def per_device(tokens, w_inner, w_keyquery, rate, grad_out):
    count = tokens.shape[0]
    width = w_inner.shape[1]
    kq_cols = w_keyquery.shape[1] * w_keyquery.shape[2]
    seqs, chans = lax.axis_size("seq"), lax.axis_size("chan")
    block = min(width, 512)
    short = seqs == 2 * ROWS and chans == ROWS and count <= w_inner.shape[0]
    plan = (Exchanged if short else Gathered)(tokens, w_inner)
    kq_parts = gathered(w_keyquery.reshape(-1, kq_cols).T, "seq")
    full_kq = side_by_side(kq_parts)
    group = lax.axis_index("chan")
    kq_rows = []
    for m in range(chans):
        rows = lax.dynamic_slice_in_dim(
            full_kq, (group + m) % chans * (full_kq.shape[1] // chans), full_kq.shape[1] // chans, 1
        )
        kq_rows.append(along_chan(rows, m))
    keyquery = dot_t(tokens, full_kq)
    keys = keyquery[:, :NS]
    sumsq = jnp.sum(keys * keys, axis=1)
    eps = rate[None, :] / (1.0 + rate[None, :] * sumsq[:, None])
    spread = jnp.broadcast_to(keyquery[:, :, None], (count, 2 * NS, LANES))
    rows_f = pltpu.VMEM((count, block), F32)
    run = functools.partial(call, tokens=count, width=width, block=block)

    (pair,) = run(
        adjoint_totals_kernel,
        ins=["kq", "rows", "rows16"], outs=["pair"], scratch=[rows_f],
        args=(spread, eps, grad_out), work=4,
    )
    end_adjoint, plan.came = carried(pair, -1, plan.came)
    beside, rest = plan.partials()
    near, far, beside = plan.spread(beside, rest)
    adjoints, inner_grad = run(
        adjoint_kernel,
        ins=["kq", "rows", "rows16", "state"], outs=["states", "rows16"], scratch=[rows_f, rows_f],
        args=(spread, eps, grad_out, end_adjoint), work=10,
    )
    beside, _ = lax.optimization_barrier((beside, inner_grad))
    inner, even, odd = plan.inner(near, far, beside, inner_grad)
    inner, kq_rows = lax.optimization_barrier((inner, jnp.concatenate(kq_rows, axis=0)))
    (alone_end,) = run(
        state_total_kernel,
        ins=["kq", "rows", "rows"], outs=["state"], scratch=[],
        args=(spread, eps, inner), work=4,
    )
    start_state, odd = carried(jnp.concatenate([alone_end, pair[NS:]], axis=0), 1, odd)
    tokens_sum, start_state = plan.grad_tokens(even, odd, start_state)
    acc = pltpu.VMEM((count, NS, LANES), F32)
    mixed, kq_grad = run(
        mixer_kernel,
        ins=["kq", "rows", "rows", "rows16", "states", "state"], outs=["rows16", "gkq"],
        scratch=[rows_f, rows_f, acc, acc],
        args=(spread, eps, inner, grad_out, adjoints, start_state), work=22,
    )
    kq_grad = kq_grad[:, :kq_cols].astype(BF16)

    all_kq = jnp.concatenate([along_chan(kq_grad, m) for m in range(chans)], axis=1)
    grad_tokens = (
        tokens_sum + jnp.dot(all_kq, kq_rows, preferred_element_type=F32)
    ).astype(BF16)

    grad_cols = lax.dot_general(
        kq_grad, tokens, (((0,), (0,)), ((), ())), preferred_element_type=F32
    )
    grad_parts = lax.all_to_all(
        jnp.moveaxis(grad_cols.astype(BF16).reshape(kq_cols, seqs, -1), 1, 0), "seq", 0, 0, tiled=True
    )
    grad_keyquery = jnp.sum(grad_parts.astype(F32), axis=0).T.reshape(w_keyquery.shape)
    return (mixed, grad_tokens, grad_keyquery)


def solution(mesh):
    return jax.shard_map(
        per_device,
        mesh=mesh,
        in_specs=(
            P("seq", None),
            P("seq", "chan"),
            P("seq", "chan", None),
            P("chan"),
            P("seq", "chan"),
        ),
        out_specs=(P("seq", "chan"), P("seq", "chan"), P("seq", "chan", None)),
        check_vma=False,
    )
```

```python
import functools

import jax
import jax.numpy as jnp
from jax import lax
from jax.experimental import pallas as pl
from jax.experimental.pallas import tpu as pltpu
from jax.sharding import PartitionSpec as P

NS = 16
LANES = 128
UNROLL = 8
ROWS = 4
WORK = 1
F32 = jnp.float32
BF16 = jnp.bfloat16


def lane_groups(width):
    return [slice(j * LANES, (j + 1) * LANES) for j in range(width // LANES)]


def tile(ref, first, cols):
    return ref[pl.ds(first, UNROLL), cols]


def place(rows, at, value):
    here = lax.broadcasted_iota(jnp.int32, rows.shape, 0) == at
    return jnp.where(here, jnp.broadcast_to(value, rows.shape), rows)


def to_float(src, dst):
    dst[...] = src[...].astype(F32)


def adjoint_totals_kernel(kq, eps, cot, pair_out, cot_f):
    tokens, width = eps.shape
    groups = lane_groups(width)
    to_float(cot, cot_f)

    def block(i, carry):
        lams, decays = carry
        first = pl.multiple_of(tokens - (i + 1) * UNROLL, UNROLL)
        steps = [tile(eps, first, cols) for cols in groups]
        cots = [tile(cot_f, first, cols) for cols in groups]
        for j in reversed(range(UNROLL)):
            t = first + j
            keys = kq[t, :NS, :]
            queries = kq[t, NS:, :]
            square = keys * keys
            new_lams, new_decays = [], []
            for lam, total, step, cot_row in zip(lams, decays, steps, cots):
                decay = 1.0 - step[j : j + 1] * square
                new_lams.append(decay * (queries * cot_row[j : j + 1] + lam))
                new_decays.append(total * decay)
            lams, decays = new_lams, new_decays
        return (tuple(lams), tuple(decays))

    zeros = tuple(jnp.zeros((NS, LANES), F32) for _ in groups)
    ones = tuple(jnp.ones((NS, LANES), F32) for _ in groups)
    lams, decays = lax.fori_loop(0, tokens // UNROLL, block, (zeros, ones))
    for lam, total, cols in zip(lams, decays, groups):
        pair_out[:NS, cols] = lam
        pair_out[NS:, cols] = total


def inner_grad_kernel(kq, eps, cot, start, grad_out, cot_f, grad_f):
    tokens, width = eps.shape
    groups = lane_groups(width)
    to_float(cot, cot_f)

    def block(i, lams):
        first = pl.multiple_of(tokens - (i + 1) * UNROLL, UNROLL)
        steps = [tile(eps, first, cols) for cols in groups]
        cots = [tile(cot_f, first, cols) for cols in groups]
        grads = [jnp.zeros((UNROLL, LANES), F32) for _ in groups]
        for j in reversed(range(UNROLL)):
            t = first + j
            keys = kq[t, :NS, :]
            queries = kq[t, NS:, :]
            square = keys * keys
            new_lams = []
            for n, cols in enumerate(groups):
                adj = queries * cots[n][j : j + 1] + lams[n]
                grads[n] = place(grads[n], j, jnp.sum(adj * keys, axis=0, keepdims=True))
                new_lams.append((1.0 - steps[n][j : j + 1] * square) * adj)
            lams = new_lams
        for n, cols in enumerate(groups):
            grad_f[pl.ds(first, UNROLL), cols] = steps[n] * grads[n]
        return tuple(lams)

    lax.fori_loop(0, tokens // UNROLL, block, tuple(start[:, cols] for cols in groups))
    grad_out[...] = grad_f[...].astype(BF16)


def adjoint_kernel(kq, eps, cot, start, adj_out, cot_f):
    tokens, width = eps.shape
    groups = lane_groups(width)
    to_float(cot, cot_f)

    def block(i, lams):
        first = pl.multiple_of(tokens - (i + 1) * UNROLL, UNROLL)
        steps = [tile(eps, first, cols) for cols in groups]
        cots = [tile(cot_f, first, cols) for cols in groups]
        for j in reversed(range(UNROLL)):
            t = first + j
            keys = kq[t, :NS, :]
            queries = kq[t, NS:, :]
            square = keys * keys
            new_lams = []
            for n, cols in enumerate(groups):
                adj = queries * cots[n][j : j + 1] + lams[n]
                adj_out[t, :, cols] = adj
                new_lams.append((1.0 - steps[n][j : j + 1] * square) * adj)
            lams = new_lams
        return tuple(lams)

    lax.fori_loop(0, tokens // UNROLL, block, tuple(start[:, cols] for cols in groups))


def state_total_kernel(kq, eps, inner, state_out):
    tokens, width = eps.shape
    groups = lane_groups(width)

    def block(i, states):
        first = pl.multiple_of(i * UNROLL, UNROLL)
        steps = [tile(eps, first, cols) for cols in groups]
        pushes = [tile(inner, first, cols) * step for cols, step in zip(groups, steps)]
        for j in range(UNROLL):
            t = first + j
            keys = kq[t, :NS, :]
            square = keys * keys
            states = [
                (1.0 - step[j : j + 1] * square) * state + push[j : j + 1] * keys
                for state, step, push in zip(states, steps, pushes)
            ]
        return tuple(states)

    zeros = tuple(jnp.zeros((NS, LANES), F32) for _ in groups)
    states = lax.fori_loop(0, tokens // UNROLL, block, zeros)
    for state, cols in zip(states, groups):
        state_out[:, cols] = state


def kq_grad_kernel(kq, eps, inner, cot, adj_in, start, gkq_out, cot_f, key_acc, query_acc):
    tokens, width = eps.shape
    groups = lane_groups(width)
    to_float(cot, cot_f)

    @pl.when(pl.program_id(0) == 0)
    def _():
        key_acc[...] = jnp.zeros_like(key_acc)
        query_acc[...] = jnp.zeros_like(query_acc)

    def block(i, states):
        first = pl.multiple_of(i * UNROLL, UNROLL)
        steps = [tile(eps, first, cols) for cols in groups]
        inners = [tile(inner, first, cols) for cols in groups]
        pushes = [step * x for step, x in zip(steps, inners)]
        squares = [step * step for step in steps]
        cots = [tile(cot_f, first, cols) for cols in groups]
        for j in range(UNROLL):
            t = first + j
            keys = kq[t, :NS, :]
            square = keys * keys
            new_states = []
            key_sum = jnp.zeros((NS, LANES), F32)
            step_sum = jnp.zeros((NS, LANES), F32)
            query_sum = jnp.zeros((NS, LANES), F32)
            for n, cols in enumerate(groups):
                step = steps[n][j : j + 1]
                adj = adj_in[t, :, cols]
                through_decay = keys * (adj * states[n])
                through_both = inners[n][j : j + 1] * adj - through_decay
                key_sum = key_sum + step * (through_both - through_decay)
                step_sum = step_sum + squares[n][j : j + 1] * through_both
                state = (1.0 - step * square) * states[n] + pushes[n][j : j + 1] * keys
                query_sum = query_sum + state * cots[n][j : j + 1]
                new_states.append(state)
            states = new_states
            through_step = jnp.sum(keys * step_sum, axis=0, keepdims=True)
            key_acc[t] += key_sum - 2.0 * keys * through_step
            query_acc[t] += query_sum
        return tuple(states)

    lax.fori_loop(0, tokens // UNROLL, block, tuple(start[:, cols] for cols in groups))

    @pl.when(pl.program_id(0) == pl.num_programs(0) - 1)
    def _():
        ones = jnp.ones((LANES, LANES), F32)
        lane = lax.broadcasted_iota(jnp.int32, (NS, LANES), 1)
        state = lax.broadcasted_iota(jnp.int32, (NS, LANES), 0)

        def spread(acc, first):
            total = jnp.dot(
                acc[...].reshape(tokens * NS, LANES),
                ones,
                preferred_element_type=F32,
                precision=lax.Precision.HIGHEST,
            )
            placed = jnp.where(
                (lane == state + first)[None], total.reshape(tokens, NS, LANES), 0.0
            )
            return jnp.sum(placed, axis=1)

        gkq_out[...] = spread(key_acc, 0) + spread(query_acc, NS)


def mixer_kernel(kq, eps, inner, start, mixed_out, mixed_f):
    tokens, width = eps.shape
    groups = lane_groups(width)

    def block(i, states):
        first = pl.multiple_of(i * UNROLL, UNROLL)
        steps = [tile(eps, first, cols) for cols in groups]
        pushes = [tile(inner, first, cols) * step for cols, step in zip(groups, steps)]
        outs = [jnp.zeros((UNROLL, LANES), F32) for _ in groups]
        for j in range(UNROLL):
            t = first + j
            keys = kq[t, :NS, :]
            queries = kq[t, NS:, :]
            square = keys * keys
            states = [
                (1.0 - step[j : j + 1] * square) * state + push[j : j + 1] * keys
                for state, step, push in zip(states, steps, pushes)
            ]
            outs = [
                place(out, j, jnp.sum(state * queries, axis=0, keepdims=True))
                for out, state in zip(outs, states)
            ]
        for out, cols in zip(outs, groups):
            mixed_f[pl.ds(first, UNROLL), cols] = out
        return tuple(states)

    lax.fori_loop(0, tokens // UNROLL, block, tuple(start[:, cols] for cols in groups))
    mixed_out[...] = mixed_f[...].astype(BF16)


def call(kernel, tokens, width, block, ins, outs, scratch, args, work):
    def spec(kind):
        return {
            "kq": pl.BlockSpec((tokens, 2 * NS, LANES), lambda c: (0, 0, 0)),
            "rows": pl.BlockSpec((tokens, block), lambda c: (0, c)),
            "rows16": pl.BlockSpec((tokens, block), lambda c: (0, c)),
            "state": pl.BlockSpec((NS, block), lambda c: (0, c)),
            "pair": pl.BlockSpec((2 * NS, block), lambda c: (0, c)),
            "states": pl.BlockSpec((tokens, NS, block), lambda c: (0, 0, c)),
            "gkq": pl.BlockSpec((tokens, LANES), lambda c: (0, 0)),
        }[kind]

    def shape(kind):
        return {
            "rows": jax.ShapeDtypeStruct((tokens, width), F32),
            "rows16": jax.ShapeDtypeStruct((tokens, width), BF16),
            "state": jax.ShapeDtypeStruct((NS, width), F32),
            "pair": jax.ShapeDtypeStruct((2 * NS, width), F32),
            "states": jax.ShapeDtypeStruct((tokens, NS, width), F32),
            "gkq": jax.ShapeDtypeStruct((tokens, LANES), F32),
        }[kind]

    return pl.pallas_call(
        kernel,
        grid=(width // block,),
        in_specs=[spec(kind) for kind in ins],
        out_specs=[spec(kind) for kind in outs],
        out_shape=[shape(kind) for kind in outs],
        scratch_shapes=scratch,
        compiler_params=pltpu.CompilerParams(vmem_limit_bytes=48 * 2**20),
        cost_estimate=pl.CostEstimate(
            flops=work * WORK * tokens * NS * width,
            bytes_accessed=1024,
            transcendentals=0,
        ),
    )(*args)


def shifted(value, axis, by):
    peers = lax.axis_size(axis)
    pairs = [(i, i + by) for i in range(peers) if 0 <= i + by < peers]
    return lax.ppermute(value, axis, pairs)


def carried(pair, sign, early=None):
    count = lax.axis_size("seq")
    window, radix = 1, 4
    total, decay = pair[:NS], pair[NS:]
    inc, exc_total, exc_decay = pair, None, None
    while window < count:
        last = window * radix >= count
        if last and window * 2 >= count:
            inc = inc[:NS]
        wire = inc.astype(BF16)
        if last and early is not None:
            wire, early = lax.optimization_barrier((wire, early))
        for j in range(1, min(radix, -(-count // window))):
            far = shifted(wire, "seq", sign * window * j).astype(F32)
            far_total, far_decay = far[:NS], far[NS:]
            if exc_total is None:
                exc_total, exc_decay = far_total, far_decay
            else:
                exc_total = exc_total + exc_decay * far_total
                if far_decay.shape[0]:
                    exc_decay = exc_decay * far_decay
        inc = jnp.concatenate([total + decay * exc_total, decay * exc_decay], axis=0)
        window *= radix
    return exc_total, early


def along_chan(value, by):
    count = lax.axis_size("chan")
    return lax.ppermute(value, "chan", [(i, (i + by) % count) for i in range(count)]) if by else value


def gathered(value, axis):
    copies = jnp.broadcast_to(value[None], (lax.axis_size(axis),) + value.shape)
    return lax.all_to_all(copies, axis, 0, 0, tiled=True)


def side_by_side(parts):
    return jnp.moveaxis(parts, 0, 1).reshape(parts.shape[1], -1)


def scatter_sum_columns(value):
    count = lax.axis_size("chan")
    index = lax.axis_index("chan")
    if count & (count - 1):
        return lax.psum_scatter(value, "chan", scatter_dimension=1, tiled=True)
    blocks = jnp.moveaxis(value.reshape(value.shape[0], count, -1), 1, 0)
    offset = 1
    while offset < count:
        pairs = blocks.reshape((-1, 2) + blocks.shape[1:])
        bit = (index // offset) % 2
        mine = lax.dynamic_index_in_dim(pairs, bit, 1, keepdims=False)
        other = lax.dynamic_index_in_dim(pairs, 1 - bit, 1, keepdims=False)
        wire = other if offset == 1 else other.astype(BF16)
        swap = [(i, i ^ offset) for i in range(count)]
        blocks = mine + lax.ppermute(wire, "chan", swap).astype(F32)
        offset *= 2
    return blocks[0]


class Gathered:
    def __init__(self, tokens, w_inner):
        self.tokens, self.came = tokens, None
        self.full = lax.all_gather(w_inner, "seq", axis=0, tiled=True)

    def partials(self):
        return None, None

    def spread(self, beside, rest):
        return jnp.dot(self.tokens, self.full, preferred_element_type=F32), None, None

    def inner(self, near, far, beside, grad):
        return near, grad, grad

    def grad_tokens(self, even, odd, before):
        return scatter_sum_columns(dot_t(even, self.full)), before


class Exchanged:
    def __init__(self, tokens, w_inner):
        self.depth, self.width = w_inner.shape
        self.count = tokens.shape[0]
        index = lax.axis_index("seq")
        self.row, self.side = index // 2, index % 2
        self.first = lax.axis_index("chan") % 2 == 0
        self.w_mine = w_inner
        self.w_other = self.trade(w_inner, "seq", 1)
        half = jnp.where(self.first, self.side, 1 - self.side)
        came = [
            self.trade(self.columns(tokens, self.row ^ m, half), "seq", 2 * m) for m in (1, 3, 2)
        ]
        self.came = jnp.concatenate(came, axis=0)
        self.near_mine = self.columns(tokens, self.row, self.side)
        self.near_other = self.columns(tokens, self.row, 1 - self.side)

    def columns(self, tokens, row, side):
        return lax.dynamic_slice_in_dim(tokens, (row * 2 + side) * self.depth, self.depth, 1)

    def trade(self, value, axis, mask):
        pairs = [(i, i ^ mask) for i in range(lax.axis_size(axis))]
        return lax.ppermute(value, axis, pairs)

    def partials(self):
        partner = self.trade(self.came, "chan", 1)
        mine = jnp.where(self.first, self.came, partner)
        other = jnp.where(self.first, partner, self.came)
        two = 2 * self.count
        beside = self.product(mine[:two], other[:two]).astype(BF16)
        return beside, (mine[two:], other[two:])

    def product(self, mine, other):
        return jnp.dot(mine, self.w_mine, preferred_element_type=F32) + jnp.dot(
            other, self.w_other, preferred_element_type=F32
        )

    def spread(self, beside, rest):
        near = self.product(self.near_mine, self.near_other)
        return near, self.product(*rest), self.trade(beside, "seq", 2)

    def inner(self, near, far, beside, grad):
        wire = (far + beside[self.count :].astype(F32)).astype(BF16)
        wire, far_grad = lax.optimization_barrier((wire, self.trade(grad, "seq", 4)))
        even = jnp.concatenate([grad, far_grad], axis=0)
        odd = self.trade(even, "seq", 2)
        total = near + beside[: self.count].astype(F32) + self.trade(wire, "seq", 4).astype(F32)
        return total, even, odd

    def grad_tokens(self, even, odd, before):
        chans = lax.axis_size("chan")
        keep = jnp.where(self.first, even, odd)
        give = jnp.where(self.first, odd, even)
        one, two = self.w_mine, self.w_other
        full = jnp.concatenate(
            [jnp.where(self.side == 0, one, two), jnp.where(self.side == 0, two, one)], axis=0
        )
        kept = dot_t(keep, full) + self.trade(dot_t(give, full), "chan", 1)
        pieces = kept.astype(BF16).reshape(2, self.count, -1)
        pieces, before = lax.optimization_barrier((pieces, before))
        y = lax.axis_index("chan") // 2
        total = None
        for m in range(2):
            piece = lax.dynamic_index_in_dim(pieces, y ^ m, 0, keepdims=False)
            route = [
                (((r * 2 + s) * chans + c), ((r ^ (c % 2 + 2 * (c // 2 ^ m))) * 2 + s) * chans + r)
                for r in range(ROWS)
                for s in range(2)
                for c in range(chans)
            ]
            piece = lax.ppermute(piece, ("seq", "chan"), route).astype(F32)
            total = piece if total is None else total + piece
        return total, before


def dot_t(left, right):
    return lax.dot_general(left, right, (((1,), (1,)), ((), ())), preferred_element_type=F32)


def per_device(tokens, w_inner, w_keyquery, rate, grad_out):
    count = tokens.shape[0]
    width = w_inner.shape[1]
    kq_cols = w_keyquery.shape[1] * w_keyquery.shape[2]
    seqs, chans = lax.axis_size("seq"), lax.axis_size("chan")
    block = min(width, 512)
    short = seqs == 2 * ROWS and chans == ROWS and count <= w_inner.shape[0]
    plan = (Exchanged if short else Gathered)(tokens, w_inner)
    kq_parts = gathered(w_keyquery.reshape(-1, kq_cols).T, "seq")
    full_kq = side_by_side(kq_parts)
    group = lax.axis_index("chan")
    kq_rows = []
    for m in range(chans):
        rows = lax.dynamic_slice_in_dim(
            full_kq, (group + m) % chans * (full_kq.shape[1] // chans), full_kq.shape[1] // chans, 1
        )
        kq_rows.append(along_chan(rows, m))
    keyquery = dot_t(tokens, full_kq)
    keys = keyquery[:, :NS]
    sumsq = jnp.sum(keys * keys, axis=1)
    eps = rate[None, :] / (1.0 + rate[None, :] * sumsq[:, None])
    spread = jnp.broadcast_to(keyquery[:, :, None], (count, 2 * NS, LANES))
    rows_f = pltpu.VMEM((count, block), F32)
    run = functools.partial(call, tokens=count, width=width, block=block)

    (pair,) = run(
        adjoint_totals_kernel,
        ins=["kq", "rows", "rows16"], outs=["pair"], scratch=[rows_f],
        args=(spread, eps, grad_out), work=4,
    )
    end_adjoint, plan.came = carried(pair, -1, plan.came)
    beside, rest = plan.partials()
    near, far, beside = plan.spread(beside, rest)
    (inner_grad,) = run(
        inner_grad_kernel,
        ins=["kq", "rows", "rows16", "state"], outs=["rows16"], scratch=[rows_f, rows_f],
        args=(spread, eps, grad_out, end_adjoint), work=8,
    )
    (adjoints,) = run(
        adjoint_kernel,
        ins=["kq", "rows", "rows16", "state"], outs=["states"], scratch=[rows_f],
        args=(spread, eps, grad_out, lax.optimization_barrier((end_adjoint, inner_grad))[0]),
        work=10,
    )
    beside, _ = lax.optimization_barrier((beside, inner_grad))
    inner, even, odd = plan.inner(near, far, beside, inner_grad)
    inner, kq_rows, adjoints = lax.optimization_barrier(
        (inner, jnp.concatenate(kq_rows, axis=0), adjoints)
    )
    (alone_end,) = run(
        state_total_kernel,
        ins=["kq", "rows", "rows"], outs=["state"], scratch=[],
        args=(spread, eps, inner), work=4,
    )
    start_state, odd = carried(jnp.concatenate([alone_end, pair[NS:]], axis=0), 1, odd)
    tokens_sum, start_state = plan.grad_tokens(even, odd, start_state)
    acc = pltpu.VMEM((count, NS, LANES), F32)
    (kq_grad,) = run(
        kq_grad_kernel,
        ins=["kq", "rows", "rows", "rows16", "states", "state"], outs=["gkq"],
        scratch=[rows_f, acc, acc],
        args=(spread, eps, inner, grad_out, adjoints, start_state), work=22,
    )
    (mixed,) = run(
        mixer_kernel,
        ins=["kq", "rows", "rows", "state"], outs=["rows16"], scratch=[rows_f],
        args=(spread, eps, inner, lax.optimization_barrier((start_state, kq_grad))[0]),
        work=8,
    )
    kq_grad = kq_grad[:, :kq_cols].astype(BF16)

    all_kq = jnp.concatenate([along_chan(kq_grad, m) for m in range(chans)], axis=1)
    grad_tokens = (
        tokens_sum + jnp.dot(all_kq, kq_rows, preferred_element_type=F32)
    ).astype(BF16)

    grad_cols = lax.dot_general(
        kq_grad, tokens, (((0,), (0,)), ((), ())), preferred_element_type=F32
    )
    grad_parts = lax.all_to_all(
        jnp.moveaxis(grad_cols.astype(BF16).reshape(kq_cols, seqs, -1), 1, 0), "seq", 0, 0, tiled=True
    )
    grad_keyquery = jnp.sum(grad_parts.astype(F32), axis=0).T.reshape(w_keyquery.shape)
    return (mixed, grad_tokens, grad_keyquery)


def solution(mesh):
    return jax.shard_map(
        per_device,
        mesh=mesh,
        in_specs=(
            P("seq", None),
            P("seq", "chan"),
            P("seq", "chan", None),
            P("chan"),
            P("seq", "chan"),
        ),
        out_specs=(P("seq", "chan"), P("seq", "chan"), P("seq", "chan", None)),
        check_vma=False,
    )
```

```python
import functools

import jax
import jax.numpy as jnp
from jax import lax
from jax.experimental import pallas as pl
from jax.experimental.pallas import tpu as pltpu
from jax.sharding import PartitionSpec as P

NS = 16
LANES = 128
UNROLL = 8
ROWS = 4
WORK = 1
F32 = jnp.float32
BF16 = jnp.bfloat16


def lane_groups(width):
    return [slice(j * LANES, (j + 1) * LANES) for j in range(width // LANES)]


def tile(ref, first, cols):
    return ref[pl.ds(first, UNROLL), cols]


def place(rows, at, value):
    here = lax.broadcasted_iota(jnp.int32, rows.shape, 0) == at
    return jnp.where(here, jnp.broadcast_to(value, rows.shape), rows)


def to_float(src, dst):
    dst[...] = src[...].astype(F32)


def adjoint_totals_kernel(kq, eps, cot, pair_out, cot_f):
    tokens, width = eps.shape
    groups = lane_groups(width)
    to_float(cot, cot_f)

    def block(i, carry):
        lams, decays = carry
        first = pl.multiple_of(tokens - (i + 1) * UNROLL, UNROLL)
        steps = [tile(eps, first, cols) for cols in groups]
        cots = [tile(cot_f, first, cols) for cols in groups]
        for j in reversed(range(UNROLL)):
            t = first + j
            keys = kq[t, :NS, :]
            queries = kq[t, NS:, :]
            square = keys * keys
            new_lams, new_decays = [], []
            for lam, total, step, cot_row in zip(lams, decays, steps, cots):
                decay = 1.0 - step[j : j + 1] * square
                new_lams.append(decay * (queries * cot_row[j : j + 1] + lam))
                new_decays.append(total * decay)
            lams, decays = new_lams, new_decays
        return (tuple(lams), tuple(decays))

    zeros = tuple(jnp.zeros((NS, LANES), F32) for _ in groups)
    ones = tuple(jnp.ones((NS, LANES), F32) for _ in groups)
    lams, decays = lax.fori_loop(0, tokens // UNROLL, block, (zeros, ones))
    for lam, total, cols in zip(lams, decays, groups):
        pair_out[:NS, cols] = lam
        pair_out[NS:, cols] = total


def inner_grad_kernel(kq, eps, cot, start, grad_out, cot_f, grad_f):
    tokens, width = eps.shape
    groups = lane_groups(width)
    to_float(cot, cot_f)

    def block(i, lams):
        first = pl.multiple_of(tokens - (i + 1) * UNROLL, UNROLL)
        steps = [tile(eps, first, cols) for cols in groups]
        cots = [tile(cot_f, first, cols) for cols in groups]
        grads = [jnp.zeros((UNROLL, LANES), F32) for _ in groups]
        for j in reversed(range(UNROLL)):
            t = first + j
            keys = kq[t, :NS, :]
            queries = kq[t, NS:, :]
            square = keys * keys
            new_lams = []
            for n, cols in enumerate(groups):
                adj = queries * cots[n][j : j + 1] + lams[n]
                grads[n] = place(grads[n], j, jnp.sum(adj * keys, axis=0, keepdims=True))
                new_lams.append((1.0 - steps[n][j : j + 1] * square) * adj)
            lams = new_lams
        for n, cols in enumerate(groups):
            grad_f[pl.ds(first, UNROLL), cols] = steps[n] * grads[n]
        return tuple(lams)

    lax.fori_loop(0, tokens // UNROLL, block, tuple(start[:, cols] for cols in groups))
    grad_out[...] = grad_f[...].astype(BF16)


def adjoint_kernel(kq, eps, cot, start, adj_out, cot_f):
    tokens, width = eps.shape
    groups = lane_groups(width)
    to_float(cot, cot_f)

    def block(i, lams):
        first = pl.multiple_of(tokens - (i + 1) * UNROLL, UNROLL)
        steps = [tile(eps, first, cols) for cols in groups]
        cots = [tile(cot_f, first, cols) for cols in groups]
        for j in reversed(range(UNROLL)):
            t = first + j
            keys = kq[t, :NS, :]
            queries = kq[t, NS:, :]
            square = keys * keys
            new_lams = []
            for n, cols in enumerate(groups):
                adj = queries * cots[n][j : j + 1] + lams[n]
                adj_out[t, :, cols] = adj
                new_lams.append((1.0 - steps[n][j : j + 1] * square) * adj)
            lams = new_lams
        return tuple(lams)

    lax.fori_loop(0, tokens // UNROLL, block, tuple(start[:, cols] for cols in groups))


def state_total_kernel(kq, eps, inner, state_out):
    tokens, width = eps.shape
    groups = lane_groups(width)

    def block(i, states):
        first = pl.multiple_of(i * UNROLL, UNROLL)
        steps = [tile(eps, first, cols) for cols in groups]
        pushes = [tile(inner, first, cols) * step for cols, step in zip(groups, steps)]
        for j in range(UNROLL):
            t = first + j
            keys = kq[t, :NS, :]
            square = keys * keys
            states = [
                (1.0 - step[j : j + 1] * square) * state + push[j : j + 1] * keys
                for state, step, push in zip(states, steps, pushes)
            ]
        return tuple(states)

    zeros = tuple(jnp.zeros((NS, LANES), F32) for _ in groups)
    states = lax.fori_loop(0, tokens // UNROLL, block, zeros)
    for state, cols in zip(states, groups):
        state_out[:, cols] = state


def kq_grad_kernel(kq, eps, inner, cot, adj_in, start, gkq_out, cot_f, key_acc, query_acc):
    tokens, width = eps.shape
    groups = lane_groups(width)
    to_float(cot, cot_f)

    @pl.when(pl.program_id(0) == 0)
    def _():
        key_acc[...] = jnp.zeros_like(key_acc)
        query_acc[...] = jnp.zeros_like(query_acc)

    def block(i, states):
        first = pl.multiple_of(i * UNROLL, UNROLL)
        steps = [tile(eps, first, cols) for cols in groups]
        inners = [tile(inner, first, cols) for cols in groups]
        pushes = [step * x for step, x in zip(steps, inners)]
        squares = [step * step for step in steps]
        cots = [tile(cot_f, first, cols) for cols in groups]
        for j in range(UNROLL):
            t = first + j
            keys = kq[t, :NS, :]
            square = keys * keys
            new_states = []
            key_sum = jnp.zeros((NS, LANES), F32)
            step_sum = jnp.zeros((NS, LANES), F32)
            query_sum = jnp.zeros((NS, LANES), F32)
            for n, cols in enumerate(groups):
                step = steps[n][j : j + 1]
                adj = adj_in[t, :, cols]
                through_decay = keys * (adj * states[n])
                through_both = inners[n][j : j + 1] * adj - through_decay
                key_sum = key_sum + step * (through_both - through_decay)
                step_sum = step_sum + squares[n][j : j + 1] * through_both
                state = (1.0 - step * square) * states[n] + pushes[n][j : j + 1] * keys
                query_sum = query_sum + state * cots[n][j : j + 1]
                new_states.append(state)
            states = new_states
            through_step = jnp.sum(keys * step_sum, axis=0, keepdims=True)
            key_acc[t] += key_sum - 2.0 * keys * through_step
            query_acc[t] += query_sum
        return tuple(states)

    lax.fori_loop(0, tokens // UNROLL, block, tuple(start[:, cols] for cols in groups))

    @pl.when(pl.program_id(0) == pl.num_programs(0) - 1)
    def _():
        ones = jnp.ones((LANES, LANES), F32)
        lane = lax.broadcasted_iota(jnp.int32, (NS, LANES), 1)
        state = lax.broadcasted_iota(jnp.int32, (NS, LANES), 0)

        def spread(acc, first):
            total = jnp.dot(
                acc[...].reshape(tokens * NS, LANES),
                ones,
                preferred_element_type=F32,
                precision=lax.Precision.HIGHEST,
            )
            placed = jnp.where(
                (lane == state + first)[None], total.reshape(tokens, NS, LANES), 0.0
            )
            return jnp.sum(placed, axis=1)

        gkq_out[...] = spread(key_acc, 0) + spread(query_acc, NS)


def mixer_kernel(kq, eps, inner, start, mixed_out, mixed_f):
    tokens, width = eps.shape
    groups = lane_groups(width)

    def block(i, states):
        first = pl.multiple_of(i * UNROLL, UNROLL)
        steps = [tile(eps, first, cols) for cols in groups]
        pushes = [tile(inner, first, cols) * step for cols, step in zip(groups, steps)]
        outs = [jnp.zeros((UNROLL, LANES), F32) for _ in groups]
        for j in range(UNROLL):
            t = first + j
            keys = kq[t, :NS, :]
            queries = kq[t, NS:, :]
            square = keys * keys
            states = [
                (1.0 - step[j : j + 1] * square) * state + push[j : j + 1] * keys
                for state, step, push in zip(states, steps, pushes)
            ]
            outs = [
                place(out, j, jnp.sum(state * queries, axis=0, keepdims=True))
                for out, state in zip(outs, states)
            ]
        for out, cols in zip(outs, groups):
            mixed_f[pl.ds(first, UNROLL), cols] = out
        return tuple(states)

    lax.fori_loop(0, tokens // UNROLL, block, tuple(start[:, cols] for cols in groups))
    mixed_out[...] = mixed_f[...].astype(BF16)


def call(kernel, tokens, width, block, ins, outs, scratch, args, work):
    def spec(kind):
        return {
            "kq": pl.BlockSpec((tokens, 2 * NS, LANES), lambda c: (0, 0, 0)),
            "rows": pl.BlockSpec((tokens, block), lambda c: (0, c)),
            "rows16": pl.BlockSpec((tokens, block), lambda c: (0, c)),
            "state": pl.BlockSpec((NS, block), lambda c: (0, c)),
            "pair": pl.BlockSpec((2 * NS, block), lambda c: (0, c)),
            "states": pl.BlockSpec((tokens, NS, block), lambda c: (0, 0, c)),
            "gkq": pl.BlockSpec((tokens, LANES), lambda c: (0, 0)),
        }[kind]

    def shape(kind):
        return {
            "rows": jax.ShapeDtypeStruct((tokens, width), F32),
            "rows16": jax.ShapeDtypeStruct((tokens, width), BF16),
            "state": jax.ShapeDtypeStruct((NS, width), F32),
            "pair": jax.ShapeDtypeStruct((2 * NS, width), F32),
            "states": jax.ShapeDtypeStruct((tokens, NS, width), F32),
            "gkq": jax.ShapeDtypeStruct((tokens, LANES), F32),
        }[kind]

    return pl.pallas_call(
        kernel,
        grid=(width // block,),
        in_specs=[spec(kind) for kind in ins],
        out_specs=[spec(kind) for kind in outs],
        out_shape=[shape(kind) for kind in outs],
        scratch_shapes=scratch,
        compiler_params=pltpu.CompilerParams(vmem_limit_bytes=48 * 2**20),
        cost_estimate=pl.CostEstimate(
            flops=work * WORK * tokens * NS * width,
            bytes_accessed=1024,
            transcendentals=0,
        ),
    )(*args)


def shifted(value, axis, by):
    peers = lax.axis_size(axis)
    pairs = [(i, i + by) for i in range(peers) if 0 <= i + by < peers]
    return lax.ppermute(value, axis, pairs)


def carried(pair, sign, early=None):
    count = lax.axis_size("seq")
    window, radix = 1, 4
    total, decay = pair[:NS], pair[NS:]
    inc, exc_total, exc_decay = pair, None, None
    while window < count:
        last = window * radix >= count
        if last and window * 2 >= count:
            inc = inc[:NS]
        wire = inc.astype(BF16)
        if last and early is not None:
            wire, early = lax.optimization_barrier((wire, early))
        for j in range(1, min(radix, -(-count // window))):
            far = shifted(wire, "seq", sign * window * j).astype(F32)
            far_total, far_decay = far[:NS], far[NS:]
            if exc_total is None:
                exc_total, exc_decay = far_total, far_decay
            else:
                exc_total = exc_total + exc_decay * far_total
                if far_decay.shape[0]:
                    exc_decay = exc_decay * far_decay
        inc = jnp.concatenate([total + decay * exc_total, decay * exc_decay], axis=0)
        window *= radix
    return exc_total, early


def along_chan(value, by):
    count = lax.axis_size("chan")
    return lax.ppermute(value, "chan", [(i, (i + by) % count) for i in range(count)]) if by else value


def gathered(value, axis):
    copies = jnp.broadcast_to(value[None], (lax.axis_size(axis),) + value.shape)
    return lax.all_to_all(copies, axis, 0, 0, tiled=True)


def side_by_side(parts):
    return jnp.moveaxis(parts, 0, 1).reshape(parts.shape[1], -1)


def scatter_sum_columns(value):
    count = lax.axis_size("chan")
    index = lax.axis_index("chan")
    if count & (count - 1):
        return lax.psum_scatter(value, "chan", scatter_dimension=1, tiled=True)
    blocks = jnp.moveaxis(value.reshape(value.shape[0], count, -1), 1, 0)
    offset = 1
    while offset < count:
        pairs = blocks.reshape((-1, 2) + blocks.shape[1:])
        bit = (index // offset) % 2
        mine = lax.dynamic_index_in_dim(pairs, bit, 1, keepdims=False)
        other = lax.dynamic_index_in_dim(pairs, 1 - bit, 1, keepdims=False)
        wire = other if offset == 1 else other.astype(BF16)
        swap = [(i, i ^ offset) for i in range(count)]
        blocks = mine + lax.ppermute(wire, "chan", swap).astype(F32)
        offset *= 2
    return blocks[0]


class Gathered:
    def __init__(self, tokens, w_inner):
        self.tokens, self.came = tokens, None
        self.full = lax.all_gather(w_inner, "seq", axis=0, tiled=True)

    def partials(self):
        return None, None

    def spread(self, beside, rest):
        return jnp.dot(self.tokens, self.full, preferred_element_type=F32), None, None

    def inner(self, near, far, beside, grad):
        return near, grad, grad

    def grad_tokens(self, even, odd, before):
        return scatter_sum_columns(dot_t(even, self.full)), before


class Exchanged:
    def __init__(self, tokens, w_inner):
        self.depth, self.width = w_inner.shape
        self.count = tokens.shape[0]
        index = lax.axis_index("seq")
        self.row, self.side = index // 2, index % 2
        self.first = lax.axis_index("chan") % 2 == 0
        self.w_mine = w_inner
        self.w_other = self.trade(w_inner, "seq", 1)
        half = jnp.where(self.first, self.side, 1 - self.side)
        came = [
            self.trade(self.columns(tokens, self.row ^ m, half), "seq", 2 * m) for m in (1, 3, 2)
        ]
        self.came = jnp.concatenate(came, axis=0)
        self.near_mine = self.columns(tokens, self.row, self.side)
        self.near_other = self.columns(tokens, self.row, 1 - self.side)

    def columns(self, tokens, row, side):
        return lax.dynamic_slice_in_dim(tokens, (row * 2 + side) * self.depth, self.depth, 1)

    def trade(self, value, axis, mask):
        pairs = [(i, i ^ mask) for i in range(lax.axis_size(axis))]
        return lax.ppermute(value, axis, pairs)

    def partials(self):
        partner = self.trade(self.came, "chan", 1)
        mine = jnp.where(self.first, self.came, partner)
        other = jnp.where(self.first, partner, self.came)
        two = 2 * self.count
        beside = self.product(mine[:two], other[:two]).astype(BF16)
        return beside, (mine[two:], other[two:])

    def product(self, mine, other):
        return jnp.dot(mine, self.w_mine, preferred_element_type=F32) + jnp.dot(
            other, self.w_other, preferred_element_type=F32
        )

    def spread(self, beside, rest):
        near = self.product(self.near_mine, self.near_other)
        return near, self.product(*rest), self.trade(beside, "seq", 2)

    def inner(self, near, far, beside, grad):
        wire = (far + beside[self.count :].astype(F32)).astype(BF16)
        wire, far_grad = lax.optimization_barrier((wire, self.trade(grad, "seq", 4)))
        even = jnp.concatenate([grad, far_grad], axis=0)
        odd = self.trade(even, "seq", 2)
        total = near + beside[: self.count].astype(F32) + self.trade(wire, "seq", 4).astype(F32)
        return total, even, odd

    def grad_tokens(self, even, odd, before):
        chans = lax.axis_size("chan")
        keep = jnp.where(self.first, even, odd)
        give = jnp.where(self.first, odd, even)
        one, two = self.w_mine, self.w_other
        full = jnp.concatenate(
            [jnp.where(self.side == 0, one, two), jnp.where(self.side == 0, two, one)], axis=0
        )
        kept = dot_t(keep, full) + self.trade(dot_t(give, full), "chan", 1)
        pieces = kept.astype(BF16).reshape(2, self.count, -1)
        pieces, before = lax.optimization_barrier((pieces, before))
        y = lax.axis_index("chan") // 2
        total = None
        for m in range(2):
            piece = lax.dynamic_index_in_dim(pieces, y ^ m, 0, keepdims=False)
            route = [
                (((r * 2 + s) * chans + c), ((r ^ (c % 2 + 2 * (c // 2 ^ m))) * 2 + s) * chans + r)
                for r in range(ROWS)
                for s in range(2)
                for c in range(chans)
            ]
            piece = lax.ppermute(piece, ("seq", "chan"), route).astype(F32)
            total = piece if total is None else total + piece
        return total, before


def dot_t(left, right):
    return lax.dot_general(left, right, (((1,), (1,)), ((), ())), preferred_element_type=F32)


def per_device(tokens, w_inner, w_keyquery, rate, grad_out):
    count = tokens.shape[0]
    width = w_inner.shape[1]
    kq_cols = w_keyquery.shape[1] * w_keyquery.shape[2]
    seqs, chans = lax.axis_size("seq"), lax.axis_size("chan")
    block = min(width, 512)
    short = seqs == 2 * ROWS and chans == ROWS and count <= w_inner.shape[0]
    plan = (Exchanged if short else Gathered)(tokens, w_inner)
    kq_parts = gathered(w_keyquery.reshape(-1, kq_cols).T, "seq")
    full_kq = side_by_side(kq_parts)
    keyquery = dot_t(tokens, full_kq)
    keys = keyquery[:, :NS]
    sumsq = jnp.sum(keys * keys, axis=1)
    eps = rate[None, :] / (1.0 + rate[None, :] * sumsq[:, None])
    spread = jnp.broadcast_to(keyquery[:, :, None], (count, 2 * NS, LANES))
    rows_f = pltpu.VMEM((count, block), F32)
    run = functools.partial(call, tokens=count, width=width, block=block)

    (pair,) = run(
        adjoint_totals_kernel,
        ins=["kq", "rows", "rows16"], outs=["pair"], scratch=[rows_f],
        args=(spread, eps, grad_out), work=4,
    )
    end_adjoint, plan.came = carried(pair, -1, plan.came)
    beside, rest = plan.partials()
    near, far, beside = plan.spread(beside, rest)
    (inner_grad,) = run(
        inner_grad_kernel,
        ins=["kq", "rows", "rows16", "state"], outs=["rows16"], scratch=[rows_f, rows_f],
        args=(spread, eps, grad_out, end_adjoint), work=8,
    )
    (adjoints,) = run(
        adjoint_kernel,
        ins=["kq", "rows", "rows16", "state"], outs=["states"], scratch=[rows_f],
        args=(spread, eps, grad_out, lax.optimization_barrier((end_adjoint, inner_grad))[0]),
        work=10,
    )
    beside, _ = lax.optimization_barrier((beside, inner_grad))
    full_kq, _ = lax.optimization_barrier((full_kq, inner_grad))
    group = lax.axis_index("chan")
    kq_rows = []
    for m in range(chans):
        rows = lax.dynamic_slice_in_dim(
            full_kq, (group + m) % chans * (full_kq.shape[1] // chans), full_kq.shape[1] // chans, 1
        )
        kq_rows.append(along_chan(rows, m))
    inner, even, odd = plan.inner(near, far, beside, inner_grad)
    inner, kq_rows, adjoints = lax.optimization_barrier(
        (inner, jnp.concatenate(kq_rows, axis=0), adjoints)
    )
    (alone_end,) = run(
        state_total_kernel,
        ins=["kq", "rows", "rows"], outs=["state"], scratch=[],
        args=(spread, eps, inner), work=4,
    )
    start_state, odd = carried(jnp.concatenate([alone_end, pair[NS:]], axis=0), 1, odd)
    tokens_sum, start_state = plan.grad_tokens(even, odd, start_state)
    acc = pltpu.VMEM((count, NS, LANES), F32)
    (kq_grad,) = run(
        kq_grad_kernel,
        ins=["kq", "rows", "rows", "rows16", "states", "state"], outs=["gkq"],
        scratch=[rows_f, acc, acc],
        args=(spread, eps, inner, grad_out, adjoints, start_state), work=22,
    )
    (mixed,) = run(
        mixer_kernel,
        ins=["kq", "rows", "rows", "state"], outs=["rows16"], scratch=[rows_f],
        args=(spread, eps, inner, lax.optimization_barrier((start_state, kq_grad))[0]),
        work=8,
    )
    kq_grad = kq_grad[:, :kq_cols].astype(BF16)

    all_kq = jnp.concatenate([along_chan(kq_grad, m) for m in range(chans)], axis=1)
    grad_tokens = (
        tokens_sum + jnp.dot(all_kq, kq_rows, preferred_element_type=F32)
    ).astype(BF16)

    grad_cols = lax.dot_general(
        kq_grad, tokens, (((0,), (0,)), ((), ())), preferred_element_type=F32
    )
    grad_parts = lax.all_to_all(
        jnp.moveaxis(grad_cols.astype(BF16).reshape(kq_cols, seqs, -1), 1, 0), "seq", 0, 0, tiled=True
    )
    grad_keyquery = jnp.sum(grad_parts.astype(F32), axis=0).T.reshape(w_keyquery.shape)
    return (mixed, grad_tokens, grad_keyquery)


def solution(mesh):
    return jax.shard_map(
        per_device,
        mesh=mesh,
        in_specs=(
            P("seq", None),
            P("seq", "chan"),
            P("seq", "chan", None),
            P("chan"),
            P("seq", "chan"),
        ),
        out_specs=(P("seq", "chan"), P("seq", "chan"), P("seq", "chan", None)),
        check_vma=False,
    )
```
